128 devices in a mesh: ctx: 32 (over z, y, core), head: 4 (over x).
Axes of the slice: x: 4, y: 4, z: 4, core: 2. Of those that a mesh axis runs over, the one named last changes fastest.
Arguments:
- span_order: int32 [32, 2], replicated, may hold values from 0 to 63, as said below
- queries: bfloat16 [16384, 512], P('ctx', 'head'), may hold values from -8 to 8
- key_rows: bfloat16 [16384, 128], P('ctx'), may hold values from -8 to 8
- value_rows: bfloat16 [16384, 128], P('ctx'), may hold values from -6 to 6
- out_grads: bfloat16 [16384, 512], P('ctx', 'head'), may hold values from -6 to 6
Outputs:
- query_grad: bfloat16 [16384, 512], P('ctx', 'head')
- key_grad: bfloat16 [16384, 128], P('ctx')
- value_grad: bfloat16 [16384, 128], P('ctx')
The draws below stay inside these ranges and needn't reach their ends.
Inputs may be any that keep to these rules, and one draw needn't show every extreme that they name: `span_order`: every span 0 to 63 stands in exactly one slot, and the two slots of a row hold spans c and 63 - c.
All inputs are finite; a program needn't handle non-finite values.
Results may differ from the reference program's by a relative error of at most 0.0079.
Values may be sent and summed in bfloat16 or wider, within the bound.
No kernel may reach another device: no remote copies, remote signals or barrier semaphores. Data moves between devices by JAX's collectives and lax.ppermute only.
A program may use at most 64 MiB of HBM per device.

```python
import jax
import jax.numpy as jnp
from jax import lax

DH = 128
GROUP = 4
SPAN = 256
SPANS = 64
TOKENS = 16384


def draw_span_order(key, part):
    key = jax.random.fold_in(key, 1)
    half_count = SPANS // 2
    first_key, second_key = jax.random.split(key)
    low_span = jax.random.permutation(first_key, half_count).astype(jnp.int32)
    high_span = (SPANS - 1 - low_span).astype(jnp.int32)
    flip_bits = jax.random.randint(second_key, (half_count,), 0, 2)
    left_slot = jnp.where(flip_bits == 1, high_span, low_span)
    right_slot = jnp.where(flip_bits == 1, low_span, high_span)
    return jnp.stack([left_slot, right_slot], axis=1).astype(jnp.int32)


def draw_queries(key, part):
    key = jax.random.fold_in(key, 2)
    first_key = jax.random.fold_in(key, 0)
    drawn = jnp.clip(jax.random.normal(first_key, (TOKENS, GROUP * DH), jnp.float32), -8.0, 8.0)
    return drawn.astype(jnp.bfloat16)


def draw_key_rows(key, part):
    key = jax.random.fold_in(key, 3)
    first_key = jax.random.fold_in(key, 0)
    drawn = jnp.clip(jax.random.normal(first_key, (TOKENS, DH), jnp.float32), -8.0, 8.0)
    return drawn.astype(jnp.bfloat16)


def levels(own_key, extent, pieces, smallest, top_value):
    factor_of, own = 1.0, jax.random.fold_in(own_key, 6)
    for dim, shards_of in pieces:
        steps = jnp.exp(jax.random.uniform(jax.random.fold_in(own, dim), (shards_of,), jnp.float32, smallest / len(pieces), top_value / len(pieces)))
        factor_of = factor_of * jnp.repeat(steps, extent[dim] // shards_of).reshape([-1 if axis == dim else 1 for axis in range(len(extent))])
    return factor_of


def bell_draw(stream_key, dims, width, most, cuts=(), held_as=jnp.bfloat16):
    gain = levels(stream_key, dims, cuts, -0.22, 0.18) if cuts else 1.0
    array = jax.random.normal(stream_key, dims, jnp.float32) * width * gain
    return jnp.minimum(jnp.maximum(array, -most), most).astype(held_as)


def setup_inputs(seed: int = 0) -> dict:
    arg_keys = jax.random.split(jax.random.key(seed), 6)
    span_order = draw_span_order(jax.random.fold_in(arg_keys[5], 71), 0)
    queries = draw_queries(jax.random.fold_in(arg_keys[5], 71), 0)
    key_rows = draw_key_rows(jax.random.fold_in(arg_keys[5], 71), 0)
    value_rows = bell_draw(arg_keys[3], (TOKENS, DH), 1.0, 6.0, ((0, 32),))
    out_grads = bell_draw(arg_keys[4], (TOKENS, GROUP * DH), 1.0, 6.0, ((0, 32), (1, 4)))
    return dict(span_order=span_order, queries=queries, key_rows=key_rows, value_rows=value_rows, out_grads=out_grads)


def row_positions(span_order):
    flat_order = span_order.reshape(-1)
    row_ids = jnp.arange(TOKENS, dtype=jnp.int32)
    return flat_order[row_ids // SPAN] * SPAN + row_ids % SPAN


def reference(span_order, queries, key_rows, value_rows, out_grads):
    row_pos = row_positions(span_order)
    score_scale = DH ** -0.5
    block_rows = 2 * SPAN
    nblocks = TOKENS // block_rows
    block_starts = jnp.arange(nblocks, dtype=jnp.int32) * block_rows
    key_acc = jnp.zeros((TOKENS, DH), jnp.float32)
    value_acc = jnp.zeros((TOKENS, DH), jnp.float32)
    head_grads = []
    for head_idx in range(GROUP):
        query_head = queries[:, head_idx * DH:(head_idx + 1) * DH]
        grad_head = out_grads[:, head_idx * DH:(head_idx + 1) * DH]

        def one_block(running, begin_at):
            key_part, value_part = running
            query_block = lax.dynamic_slice_in_dim(query_head, begin_at, block_rows, 0)
            grad_block = lax.dynamic_slice_in_dim(grad_head, begin_at, block_rows, 0)
            pos_block = lax.dynamic_slice_in_dim(row_pos, begin_at, block_rows, 0)
            visible = pos_block[:, None] >= row_pos[None, :]
            scores = jnp.dot(query_block, key_rows.T, preferred_element_type=jnp.float32) * score_scale
            masked = jnp.where(visible, scores, -jnp.inf)
            row_top = jnp.max(masked, axis=1, keepdims=True)
            log_norm = row_top + jnp.log(jnp.sum(jnp.exp(masked - row_top), axis=1, keepdims=True))
            attn_probs = jnp.exp(masked - log_norm)
            dprobs = jnp.dot(grad_block, value_rows.T, preferred_element_type=jnp.float32)
            row_delta = jnp.sum(attn_probs * dprobs, axis=1, keepdims=True)
            dscores = (attn_probs * (dprobs - row_delta)).astype(jnp.bfloat16)
            dq_block = (jnp.dot(dscores, key_rows, preferred_element_type=jnp.float32) * score_scale).astype(jnp.bfloat16)
            key_part = key_part + jnp.dot(dscores.T, query_block, preferred_element_type=jnp.float32)
            value_part = value_part + jnp.dot(attn_probs.astype(jnp.bfloat16).T, grad_block, preferred_element_type=jnp.float32)
            return (key_part, value_part), dq_block

        (key_acc, value_acc), dq_blocks = lax.scan(one_block, (key_acc, value_acc), block_starts)
        head_grads.append(dq_blocks.reshape(TOKENS, DH))
    query_grad = jnp.concatenate(head_grads, axis=1)
    key_grad = (key_acc * score_scale).astype(jnp.bfloat16)
    value_grad = value_acc.astype(jnp.bfloat16)
    return (query_grad, key_grad, value_grad)
```

```python
import functools

import jax
import jax.numpy as jnp
from jax import lax
from jax.experimental import pallas as pl
from jax.experimental.pallas import tpu as pltpu
from jax.sharding import Mesh, PartitionSpec as P

DH = 128
SPAN = 256
HALF = 32
SCALE = DH ** (-0.5)
LOG2E = 1.4426950408889634
SCALE2 = SCALE * LOG2E
NEG = -1e30
NT = (((1,), (1,)), ((), ()))
NN = (((1,), (0,)), ((), ()))
F32 = jnp.float32
BF16 = jnp.bfloat16


def low_span(order_ref, z, y, c):
    row = (z * 4 + y) * 2 + c
    return jnp.minimum(order_ref[row, 0], order_ref[row, 1])


def pair_picks(order_ref, a):
    z, y, c = lax.axis_index("z"), lax.axis_index("y"), lax.axis_index("c")
    mine = low_span(order_ref, z, (y + 4 - a % 4) % 4, (c + a // 4) % 2)
    return [
        jnp.where(mine > low_span(order_ref, (z + 4 - b) % 4, y, c), 0, 1) for b in range(4)
    ]


def half(ref, piece, which, second):
    begin = which * SPAN + second * 2 * SPAN
    if not isinstance(begin, int):
        begin = pl.multiple_of(begin, SPAN)
    return ref[piece, pl.ds(begin, SPAN), :]


def products(q_ref, kv_ref, a, q_which, b, k_which):
    scores = lax.dot_general(
        half(kv_ref, b, k_which, 0), half(q_ref, a, q_which, 0), NT, preferred_element_type=F32
    )
    dprobs = lax.dot_general(
        half(kv_ref, b, k_which, 1), half(q_ref, a, q_which, 1), NT, preferred_element_type=F32
    )
    return scores * SCALE2, dprobs


def diagonal_visible():
    key_row = lax.broadcasted_iota(jnp.int32, (SPAN, SPAN), 0)
    query_row = lax.broadcasted_iota(jnp.int32, (SPAN, SPAN), 1)
    return key_row <= query_row


def for_each_pair(order_ref, tile):
    picks = pair_picks(order_ref, 0)
    tile(0, 1, [(b, 0) for b in range(4)], False)
    for b in range(1, 4):
        tile(0, picks[b], [(b, picks[b])], False)
    tile(0, 0, [(0, 0)], True)
    tile(0, 1, [(0, 1)], True)

    def one_piece(a, carry):
        picks = pair_picks(order_ref, a)
        tile(a, 1, [(b, 0) for b in range(4)], False)
        for b in range(4):
            tile(a, picks[b], [(b, picks[b])], False)
        return carry

    lax.fori_loop(1, 8, one_piece, 0)


def stats_kernel(order_ref, q_ref, kv_ref, own_ref, swapped_ref, top_ref, total_ref, weighted_ref):
    top_ref[...] = jnp.full(top_ref.shape, NEG, F32)
    total_ref[...] = jnp.zeros(total_ref.shape, F32)
    weighted_ref[...] = jnp.zeros(weighted_ref.shape, F32)

    def tile(a, q_which, keys, masked):
        slot = a * 2 + q_which
        old = top_ref[slot]
        top = old
        parts = []
        for b, k_which in keys:
            scores, dprobs = products(q_ref, kv_ref, a, q_which, b, k_which)
            if masked:
                scores = jnp.where(diagonal_visible(), scores, NEG)
            parts.append((scores.reshape(32, 8, SPAN), dprobs.reshape(32, 8, SPAN)))
            top = jnp.maximum(top, jnp.max(parts[-1][0], axis=0))
        shrink = jnp.exp2(old - top)
        total = total_ref[slot] * shrink
        weighted = weighted_ref[slot] * shrink
        for scores, dprobs in parts:
            expon = jnp.exp2(scores - top[None])
            if masked:
                expon = jnp.where(diagonal_visible().reshape(32, 8, SPAN), expon, 0.0)
            total = total + jnp.sum(expon, axis=0)
            weighted = weighted + jnp.sum(expon * dprobs, axis=0)
        top_ref[slot] = top
        total_ref[slot] = total
        weighted_ref[slot] = weighted

    for_each_pair(order_ref, tile)
    for slot in range(16):
        tops = top_ref[slot]
        top = jnp.max(tops, axis=0, keepdims=True)
        factor = jnp.exp2(tops - top)
        rows = (
            top,
            jnp.sum(total_ref[slot] * factor, axis=0, keepdims=True),
            jnp.sum(weighted_ref[slot] * factor, axis=0, keepdims=True),
        )
        other = (slot + 8) % 16
        for kind, row in enumerate(rows):
            own_ref[kind, pl.ds(slot, 1), :] = row
            swapped_ref[kind, pl.ds(other, 1), :] = row


def grads_kernel(
    order_ref, s0_ref, s1_ref, s2_ref, s3_ref, q_ref, kv_ref,
    dkv0_ref, dkv1_ref, dkv2_ref, dkv3_ref, dq_keep_ref, dq_send_ref,
    norm_ref, delta_ref, dk_ref, dv_ref, dqt_ref, kt_ref,
):
    for a in range(8):
        dc, dy = a // 4, a % 4
        found = []
        for k, ref in enumerate((s0_ref, s1_ref, s2_ref, s3_ref)):
            begin = 2 * (4 * dc + (dy - k) % 4)
            found.append([ref[kind, pl.ds(begin, 2), :] for kind in range(3)])
        top = functools.reduce(jnp.maximum, [f[0] for f in found])
        factors = [jnp.exp2(f[0] - top) for f in found]
        total = sum(f[1] * g for f, g in zip(found, factors))
        weighted = sum(f[2] * g for f, g in zip(found, factors))
        norm = top + jnp.log2(total)
        delta = weighted / total
        for which in range(2):
            norm_ref[2 * a + which] = jnp.broadcast_to(norm[which : which + 1], (8, SPAN))
            delta_ref[2 * a + which] = jnp.broadcast_to(delta[which : which + 1], (8, SPAN))
    for b in range(4):
        for which in range(2):
            kt_ref[2 * b + which] = half(kv_ref, b, which, 0).T
    dk_ref[...] = jnp.zeros(dk_ref.shape, F32)
    dv_ref[...] = jnp.zeros(dv_ref.shape, F32)
    dqt_ref[...] = jnp.zeros(dqt_ref.shape, F32)

    def tile(a, q_which, keys, masked):
        slot = a * 2 + q_which
        norm = norm_ref[slot][None]
        delta = delta_ref[slot][None]
        queries = half(q_ref, a, q_which, 0)
        out_grads = half(q_ref, a, q_which, 1)
        dqt = None
        for b, k_which in keys:
            scores, dprobs = products(q_ref, kv_ref, a, q_which, b, k_which)
            probs = jnp.exp2(scores.reshape(32, 8, SPAN) - norm)
            if masked:
                probs = jnp.where(diagonal_visible().reshape(32, 8, SPAN), probs, 0.0)
            dscores = probs * (dprobs.reshape(32, 8, SPAN) - delta)
            probs = probs.reshape(SPAN, SPAN).astype(BF16)
            dscores = dscores.reshape(SPAN, SPAN).astype(BF16)
            key_slot = 2 * b + k_which
            dv_ref[key_slot] += lax.dot_general(probs, out_grads, NN, preferred_element_type=F32)
            dk_ref[key_slot] += lax.dot_general(dscores, queries, NN, preferred_element_type=F32)
            term = lax.dot_general(kt_ref[key_slot], dscores, NN, preferred_element_type=F32)
            dqt = term if dqt is None else dqt + term
        dqt_ref[slot] += dqt

    for_each_pair(order_ref, tile)
    for b, ref in enumerate((dkv0_ref, dkv1_ref, dkv2_ref, dkv3_ref)):
        for which in range(2):
            ref[pl.ds(which * SPAN, SPAN), :] = dk_ref[2 * b + which].astype(ref.dtype)
            ref[pl.ds((2 + which) * SPAN, SPAN), :] = dv_ref[2 * b + which].astype(ref.dtype)
    for slot in range(8):
        dq_keep_ref[pl.ds(slot * SPAN, SPAN), :] = dqt_ref[slot].T.astype(dq_keep_ref.dtype)
        dq_send_ref[pl.ds(slot * SPAN, SPAN), :] = dqt_ref[slot + 8].T.astype(dq_send_ref.dtype)


SMEM = pl.BlockSpec(memory_space=pltpu.SMEM)
VMEM = pl.BlockSpec(memory_space=pltpu.VMEM)
PIECE = 4 * SPAN


def call_stats(span_order, q_all, kv_all):
    shape = jax.ShapeDtypeStruct((3, 16, SPAN), F32)
    return pl.pallas_call(
        stats_kernel,
        out_shape=(shape, shape),
        in_specs=[SMEM, VMEM, VMEM],
        out_specs=(VMEM, VMEM),
        scratch_shapes=[pltpu.VMEM((16, 8, SPAN), F32)] * 3,
        compiler_params=pltpu.CompilerParams(vmem_limit_bytes=32 * 2**20),
        cost_estimate=pl.CostEstimate(
            flops=65 * 2 * 2 * SPAN * SPAN * DH, bytes_accessed=3 * 2**20, transcendentals=65 * SPAN * SPAN
        ),
        name="stats",
    )(span_order, q_all, kv_all)


def call_grads(span_order, stats, q_all, kv_all):
    piece = jax.ShapeDtypeStruct((PIECE, DH), BF16)
    return pl.pallas_call(
        grads_kernel,
        out_shape=(
            jax.ShapeDtypeStruct((PIECE, DH), F32), piece, piece, piece,
            jax.ShapeDtypeStruct((8 * SPAN, DH), F32),
            jax.ShapeDtypeStruct((8 * SPAN, DH), BF16),
        ),
        in_specs=[SMEM] + [VMEM] * 6,
        out_specs=(VMEM,) * 6,
        scratch_shapes=[
            pltpu.VMEM((16, 8, SPAN), F32),
            pltpu.VMEM((16, 8, SPAN), F32),
            pltpu.VMEM((8, SPAN, DH), F32),
            pltpu.VMEM((8, SPAN, DH), F32),
            pltpu.VMEM((16, DH, SPAN), F32),
            pltpu.VMEM((8, DH, SPAN), BF16),
        ],
        compiler_params=pltpu.CompilerParams(vmem_limit_bytes=40 * 2**20),
        cost_estimate=pl.CostEstimate(
            flops=65 * 5 * 2 * SPAN * SPAN * DH, bytes_accessed=6 * 2**20, transcendentals=65 * SPAN * SPAN
        ),
        name="grads",
    )(span_order, *stats, q_all, kv_all)


def back(value, axis, k):
    return lax.ppermute(value, axis, [(i, (i + k) % 4) for i in range(4)])


def ahead(value, axis, k):
    return lax.ppermute(value, axis, [(i, (i - k) % 4) for i in range(4)])


def swap_core(value):
    return lax.ppermute(value, "c", [(0, 1), (1, 0)])


def local(span_order, queries, key_rows, value_rows, out_grads):
    z, y, c = lax.axis_index("z"), lax.axis_index("y"), lax.axis_index("c")
    row = (z * 4 + y) * 2 + c
    flipped = lax.dynamic_slice(span_order, (row, 0), (1, 1))[0, 0] >= HALF

    def in_order(value):
        low, high = value[:SPAN], value[SPAN:]
        return [jnp.where(flipped, high, low), jnp.where(flipped, low, high)]

    q_own = jnp.concatenate(in_order(queries) + in_order(out_grads), axis=0)
    kv_own = jnp.concatenate(in_order(key_rows) + in_order(value_rows), axis=0)
    q_near = jnp.concatenate([q_own] + [back(q_own, "y", k) for k in (1, 2, 3)], axis=0)
    kv_all = jnp.stack([kv_own] + [back(kv_own, "z", k) for k in (1, 2, 3)])
    q_all = jnp.concatenate([q_near, swap_core(q_near)], axis=0).reshape(8, PIECE, DH)

    mine, for_other = call_stats(span_order, q_all, kv_all)
    theirs = swap_core(for_other)
    top = jnp.maximum(mine[0], theirs[0])
    mine_by, theirs_by = jnp.exp2(mine[0] - top), jnp.exp2(theirs[0] - top)
    both = jnp.stack([top, mine[1] * mine_by + theirs[1] * theirs_by, mine[2] * mine_by + theirs[2] * theirs_by])
    stats = [both] + [back(both, "y", k) for k in (1, 2, 3)]

    dkv0, dkv1, dkv2, dkv3, dq_keep, dq_send = call_grads(span_order, stats, q_all, kv_all)
    zs = [ahead(part, "z", k) for k, part in ((1, dkv1), (2, dkv2), (3, dkv3))]
    dq_other = swap_core(dq_send)

    def dq_piece(k):
        rows = slice(k * 2 * SPAN, (k + 1) * 2 * SPAN)
        return dq_keep[rows] + dq_other[rows].astype(F32)

    ys = [ahead(dq_piece(k).astype(BF16), "y", k) for k in (1, 2, 3)]
    summed = (dkv0 + sum(part.astype(F32) for part in zs)).astype(BF16)
    x1, x2, x3 = [back(summed, "x", k).astype(F32) for k in (1, 2, 3)]
    total = (summed.astype(F32) + x2) + (x1 + x3)
    dq = dq_piece(0) + sum(part.astype(F32) for part in ys)

    def out_order(value):
        return jnp.concatenate(in_order(value), axis=0).astype(BF16)

    return (
        out_order(dq * SCALE),
        out_order(total[: 2 * SPAN] * SCALE),
        out_order(total[2 * SPAN :]),
    )


def solution(mesh):
    fine = Mesh(mesh.devices.reshape(4, 4, 2, 4), ("z", "y", "c", "x"))
    ctx = ("z", "y", "c")
    return jax.shard_map(
        local,
        mesh=fine,
        in_specs=(P(), P(ctx, "x"), P(ctx, None), P(ctx, None), P(ctx, "x")),
        out_specs=(P(ctx, "x"), P(ctx, None), P(ctx, None)),
        check_vma=False,
    )
```

```python
import functools

import jax
import jax.numpy as jnp
from jax import lax
from jax.experimental import pallas as pl
from jax.experimental.pallas import tpu as pltpu
from jax.sharding import Mesh, PartitionSpec as P

DH = 128
SPAN = 256
SCALE = DH ** (-0.5)
LOG2E = 1.4426950408889634
SCALE2 = SCALE * LOG2E
NEG = -1e30
NT = (((1,), (1,)), ((), ()))
NN = (((1,), (0,)), ((), ()))
F32 = jnp.float32
BF16 = jnp.bfloat16


def spans_of(order_ref, z, y, c):
    row = (z * 4 + y) * 2 + c
    first, second = order_ref[row, 0], order_ref[row, 1]
    return jnp.minimum(first, second), jnp.where(first < second, 0, 1)


def query_spans(order_ref, a):
    z, y, c = lax.axis_index("z"), lax.axis_index("y"), lax.axis_index("c")
    return spans_of(order_ref, z, (y + 4 - a % 4) % 4, (c + a // 4) % 2)


def key_spans(order_ref, b):
    z, y, c = lax.axis_index("z"), lax.axis_index("y"), lax.axis_index("c")
    return spans_of(order_ref, (z + 4 - b) % 4, y, c)


def one_query_piece(order_ref, tile, a, pieces, own):
    low, low_slot = query_spans(order_ref, a)
    found = [key_spans(order_ref, b) for b in pieces]
    tile(a, 1 - low_slot, [(b, slot) for b, (_, slot) in zip(pieces, found)], False)
    for b, (key_low, key_slot) in zip(pieces, found):
        if own and b == 0:
            tile(0, 0, [(0, 0)], True)
            tile(0, 1, [(0, 1)], True)
        else:
            lows = low > key_low
            tile(a, jnp.where(lows, low_slot, 1 - low_slot), [(b, jnp.where(lows, key_slot, 1 - key_slot))], False)


def half(ref, piece, which, second):
    begin = which * SPAN + second * 2 * SPAN
    if not isinstance(begin, int):
        begin = pl.multiple_of(begin, SPAN)
    return ref[piece, pl.ds(begin, SPAN), :]


def products(q_ref, kv_ref, a, q_which, b, k_which):
    scores = lax.dot_general(
        half(kv_ref, b, k_which, 0), half(q_ref, a, q_which, 0), NT, preferred_element_type=F32
    )
    dprobs = lax.dot_general(
        half(kv_ref, b, k_which, 1), half(q_ref, a, q_which, 1), NT, preferred_element_type=F32
    )
    return scores * SCALE2, dprobs


def diagonal_visible():
    key_row = lax.broadcasted_iota(jnp.int32, (SPAN, SPAN), 0)
    query_row = lax.broadcasted_iota(jnp.int32, (SPAN, SPAN), 1)
    return key_row <= query_row


def stats_kernel(
    order_ref, near_ref, far_ref, kv0_ref, kv1_ref, kv2_ref, kv3_ref, own_ref, swapped_ref,
    q_ref, kv_ref, top_ref, total_ref, weighted_ref,
):
    q_ref[0:4] = near_ref[...].reshape(4, PIECE, DH)
    q_ref[4:8] = far_ref[...].reshape(4, PIECE, DH)
    for b, ref in enumerate((kv0_ref, kv1_ref, kv2_ref, kv3_ref)):
        kv_ref[b] = ref[...]
    top_ref[...] = jnp.full(top_ref.shape, NEG, F32)
    total_ref[...] = jnp.zeros(total_ref.shape, F32)
    weighted_ref[...] = jnp.zeros(weighted_ref.shape, F32)

    def tile(a, q_which, keys, masked):
        slot = a * 2 + q_which
        old = top_ref[slot]
        top = old
        parts = []
        for b, k_which in keys:
            scores, dprobs = products(q_ref, kv_ref, a, q_which, b, k_which)
            if masked:
                scores = jnp.where(diagonal_visible(), scores, NEG)
            parts.append((scores.reshape(32, 8, SPAN), dprobs.reshape(32, 8, SPAN)))
            top = jnp.maximum(top, jnp.max(parts[-1][0], axis=0))
        shrink = jnp.exp2(old - top)
        total = total_ref[slot] * shrink
        weighted = weighted_ref[slot] * shrink
        for scores, dprobs in parts:
            expon = jnp.exp2(scores - top[None])
            if masked:
                expon = jnp.where(diagonal_visible().reshape(32, 8, SPAN), expon, 0.0)
            total = total + jnp.sum(expon, axis=0)
            weighted = weighted + jnp.sum(expon * dprobs, axis=0)
        top_ref[slot] = top
        total_ref[slot] = total
        weighted_ref[slot] = weighted

    pieces = (0, 1, 2, 3)
    one_query_piece(order_ref, tile, 0, pieces, True)

    def one(a, carry):
        one_query_piece(order_ref, tile, a, pieces, False)
        return carry

    lax.fori_loop(1, 8, one, 0)
    for slot in range(16):
        tops = top_ref[slot]
        top = jnp.max(tops, axis=0, keepdims=True)
        factor = jnp.exp2(tops - top)
        rows = (
            top,
            jnp.sum(total_ref[slot] * factor, axis=0, keepdims=True),
            jnp.sum(weighted_ref[slot] * factor, axis=0, keepdims=True),
        )
        other = (slot + 8) % 16
        for kind, row in enumerate(rows):
            own_ref[kind, pl.ds(slot, 1), :] = row
            swapped_ref[kind, pl.ds(other, 1), :] = row


def norm_and_delta(stat_refs, norm_ref, delta_ref):
    for a in range(8):
        dc, dy = a // 4, a % 4
        found = []
        for k, ref in enumerate(stat_refs):
            begin = 2 * (4 * dc + (dy - k) % 4)
            found.append([ref[kind, pl.ds(begin, 2), :] for kind in range(3)])
        top = functools.reduce(jnp.maximum, [f[0] for f in found])
        factors = [jnp.exp2(f[0] - top) for f in found]
        total = sum(f[1] * g for f, g in zip(found, factors))
        weighted = sum(f[2] * g for f, g in zip(found, factors))
        norm = top + jnp.log2(total)
        delta = weighted / total
        for which in range(2):
            norm_ref[2 * a + which] = jnp.broadcast_to(norm[which : which + 1], (8, SPAN))
            delta_ref[2 * a + which] = jnp.broadcast_to(delta[which : which + 1], (8, SPAN))


def grads_kernel(pieces, first, last, *refs):
    refs = list(refs)
    order_ref, stat_refs, near_ref, far_ref = refs[0], refs[1:5], refs[5], refs[6]
    del refs[:7]
    kv_refs = refs[: len(pieces)]
    del refs[: len(pieces)]
    dqt_in = None if first else refs.pop(0)
    dkv_refs = dict(zip(pieces, refs[: len(pieces)]))
    del refs[: len(pieces)]
    dq_outs = [refs.pop(0), refs.pop(0)] if last else [refs.pop(0)]
    q_ref, kv_ref, norm_ref, delta_ref, dk_ref, dv_ref, kt_ref = refs[:7]
    dqt_ref = refs[7] if last else dq_outs[0]

    norm_and_delta(stat_refs, norm_ref, delta_ref)
    q_ref[0:4] = near_ref[...].reshape(4, PIECE, DH)
    q_ref[4:8] = far_ref[...].reshape(4, PIECE, DH)
    for i, b in enumerate(pieces):
        kv_ref[i] = kv_refs[i][...]
        for which in range(2):
            kt_ref[2 * i + which] = kv_ref[i, pl.ds(which * SPAN, SPAN), :].T
    dk_ref[...] = jnp.zeros(dk_ref.shape, F32)
    dv_ref[...] = jnp.zeros(dv_ref.shape, F32)
    if first:
        dqt_ref[...] = jnp.zeros(dqt_ref.shape, F32)
    else:
        dqt_ref[...] = dqt_in[...]

    def tile(a, q_which, keys, masked):
        slot = a * 2 + q_which
        norm = norm_ref[slot][None]
        delta = delta_ref[slot][None]
        queries = half(q_ref, a, q_which, 0)
        out_grads = half(q_ref, a, q_which, 1)
        dqt = None
        for b, k_which in keys:
            i = pieces.index(b)
            key_slot = 2 * i + k_which
            scores = lax.dot_general(
                half(kv_ref, i, k_which, 0), queries, NT, preferred_element_type=F32
            ) * SCALE2
            dprobs = lax.dot_general(
                half(kv_ref, i, k_which, 1), out_grads, NT, preferred_element_type=F32
            )
            probs = jnp.exp2(scores.reshape(32, 8, SPAN) - norm)
            if masked:
                probs = jnp.where(diagonal_visible().reshape(32, 8, SPAN), probs, 0.0)
            dscores = probs * (dprobs.reshape(32, 8, SPAN) - delta)
            probs = probs.reshape(SPAN, SPAN).astype(BF16)
            dscores = dscores.reshape(SPAN, SPAN).astype(BF16)
            dv_ref[key_slot] += lax.dot_general(probs, out_grads, NN, preferred_element_type=F32)
            dk_ref[key_slot] += lax.dot_general(dscores, queries, NN, preferred_element_type=F32)
            term = lax.dot_general(kt_ref[key_slot], dscores, NN, preferred_element_type=F32)
            dqt = term if dqt is None else dqt + term
        dqt_ref[slot] += dqt

    start, step = 0, max(1, 4 // len(pieces))
    if 0 in pieces:
        one_query_piece(order_ref, tile, 0, pieces, True)
        one_query_piece(order_ref, tile, 1, pieces, False)
        start, step = 2, 3

    def some(i, carry):
        for j in range(step):
            one_query_piece(order_ref, tile, start + i * step + j, pieces, False)
        return carry

    lax.fori_loop(0, (8 - start) // step, some, 0)
    for i, b in enumerate(pieces):
        ref = dkv_refs[b]
        for which in range(2):
            ref[pl.ds(which * SPAN, SPAN), :] = dk_ref[2 * i + which].astype(ref.dtype)
            ref[pl.ds((2 + which) * SPAN, SPAN), :] = dv_ref[2 * i + which].astype(ref.dtype)
    if last:
        for out, begin in zip(dq_outs, (0, 8)):
            for slot in range(8):
                out[pl.ds(slot * SPAN, SPAN), :] = dqt_ref[begin + slot].T.astype(out.dtype)


def pack_kernel(queries_ref, keys_ref, values_ref, grads_ref, q_ref, kv_ref, sems):
    rows = 2 * SPAN
    copies = []
    for i, (source, target) in enumerate(
        ((queries_ref, q_ref), (grads_ref, q_ref), (keys_ref, kv_ref), (values_ref, kv_ref))
    ):
        place = target.at[pl.ds((i % 2) * rows, rows), :]
        copies.append(pltpu.make_async_copy(source, place, sems.at[i]))
    for copy in copies:
        copy.start()
    for copy in copies:
        copy.wait()


def middle_kernel(dkv_ref, z1_ref, z2_ref, z3_ref, sum_ref):
    total = dkv_ref[...] + z1_ref[...].astype(F32) + z2_ref[...].astype(F32) + z3_ref[...].astype(F32)
    sum_ref[...] = total.astype(BF16)


def query_kernel(keep_ref, other_ref, dq_ref, r1_ref, r2_ref, r3_ref):
    for k, ref in enumerate((dq_ref, r1_ref, r2_ref, r3_ref)):
        rows = pl.ds(k * 2 * SPAN, 2 * SPAN)
        ref[...] = (keep_ref[rows, :] + other_ref[rows, :].astype(F32)).astype(ref.dtype)


def last_kernel(sum_ref, x1_ref, x2_ref, x3_ref, dq_ref, y1_ref, y2_ref, y3_ref, q_out, k_out, v_out):
    own, x1, x2, x3 = [ref[...].astype(F32) for ref in (sum_ref, x1_ref, x2_ref, x3_ref)]
    total = (own + x2) + (x1 + x3)
    k_out[...] = (total[: 2 * SPAN] * SCALE).astype(BF16)
    v_out[...] = total[2 * SPAN :].astype(BF16)
    dq = dq_ref[...]
    for ref in (y1_ref, y2_ref, y3_ref):
        dq = dq + ref[...].astype(F32)
    q_out[...] = (dq * SCALE).astype(BF16)


SMEM = pl.BlockSpec(memory_space=pltpu.SMEM)
VMEM = pl.BlockSpec(memory_space=pltpu.VMEM)
PIECE = 4 * SPAN


def call_stats(span_order, q_near, q_far, kvs):
    shape = jax.ShapeDtypeStruct((3, 16, SPAN), F32)
    return pl.pallas_call(
        stats_kernel,
        out_shape=(shape, shape),
        in_specs=[SMEM] + [VMEM] * 6,
        out_specs=(VMEM, VMEM),
        scratch_shapes=[pltpu.VMEM((8, PIECE, DH), BF16), pltpu.VMEM((4, PIECE, DH), BF16)]
        + [pltpu.VMEM((16, 8, SPAN), F32)] * 3,
        compiler_params=pltpu.CompilerParams(vmem_limit_bytes=32 * 2**20),
        cost_estimate=pl.CostEstimate(
            flops=65 * 2 * 2 * SPAN * SPAN * DH, bytes_accessed=3 * 2**20, transcendentals=65 * SPAN * SPAN
        ),
        name="stats",
    )(span_order, q_near, q_far, *kvs)


def call_grads(pieces, first, last, span_order, stats, q_near, q_far, kvs, dqt):
    tiles = 16 * len(pieces)
    dkv_shapes = tuple(jax.ShapeDtypeStruct((PIECE, DH), BF16 if b else F32) for b in pieces)
    if last:
        dq_shapes = tuple(jax.ShapeDtypeStruct((8 * SPAN, DH), dtype) for dtype in (F32, BF16))
    else:
        dq_shapes = (jax.ShapeDtypeStruct((16, DH, SPAN), F32),)
    args = [span_order, *stats, q_near, q_far, *[kvs[b] for b in pieces]] + ([] if first else [dqt])
    out = pl.pallas_call(
        functools.partial(grads_kernel, pieces, first, last),
        out_shape=dkv_shapes + dq_shapes,
        in_specs=[SMEM] + [VMEM] * (len(args) - 1),
        out_specs=(VMEM,) * (len(pieces) + len(dq_shapes)),
        scratch_shapes=[
            pltpu.VMEM((8, PIECE, DH), BF16),
            pltpu.VMEM((len(pieces), PIECE, DH), BF16),
            pltpu.VMEM((16, 8, SPAN), F32),
            pltpu.VMEM((16, 8, SPAN), F32),
            pltpu.VMEM((2 * len(pieces), SPAN, DH), F32),
            pltpu.VMEM((2 * len(pieces), SPAN, DH), F32),
            pltpu.VMEM((2 * len(pieces), DH, SPAN), BF16),
        ]
        + ([pltpu.VMEM((16, DH, SPAN), F32)] if last else []),
        compiler_params=pltpu.CompilerParams(vmem_limit_bytes=32 * 2**20),
        cost_estimate=pl.CostEstimate(
            flops=tiles * 5 * 2 * SPAN * SPAN * DH, bytes_accessed=4 * 2**20, transcendentals=tiles * SPAN * SPAN
        ),
        name="grads",
    )(*args)
    return out[: len(pieces)], out[len(pieces) :]


def plain_call(kernel, name, out_shapes, *args):
    return pl.pallas_call(
        kernel,
        out_shape=tuple(jax.ShapeDtypeStruct(shape, dtype) for shape, dtype in out_shapes),
        in_specs=[VMEM] * len(args),
        out_specs=(VMEM,) * len(out_shapes),
        compiler_params=pltpu.CompilerParams(vmem_limit_bytes=16 * 2**20),
        cost_estimate=pl.CostEstimate(flops=2**20, bytes_accessed=2**21, transcendentals=0),
        name=name,
    )(*args)


def call_pack(*args):
    return pl.pallas_call(
        pack_kernel,
        out_shape=(jax.ShapeDtypeStruct((PIECE, DH), BF16),) * 2,
        in_specs=[pl.BlockSpec(memory_space=pl.ANY)] * 4,
        out_specs=(VMEM, VMEM),
        scratch_shapes=[pltpu.SemaphoreType.DMA((4,))],
        compiler_params=pltpu.CompilerParams(vmem_limit_bytes=56 * 2**20),
        name="pack",
    )(*args)


def back(value, axis, k):
    return lax.ppermute(value, axis, [(i, (i + k) % 4) for i in range(4)])


def ahead(value, axis, k):
    return lax.ppermute(value, axis, [(i, (i - k) % 4) for i in range(4)])


def swap_core(value):
    return lax.ppermute(value, "c", [(0, 1), (1, 0)])


def local(span_order, queries, key_rows, value_rows, out_grads):
    q_own, kv_own = call_pack(queries, key_rows, value_rows, out_grads)
    q_got = [back(q_own, "y", k) for k in (1, 2, 3)]
    kv_got = [back(kv_own, "z", k) for k in (1, 2, 3)]
    q_got, kv_got = lax.optimization_barrier((q_got, kv_got))
    q_near = jnp.concatenate([q_own] + q_got, axis=0)
    q_far = swap_core(q_near)
    kvs = [kv_own] + kv_got

    mine, for_other = call_stats(span_order, q_near, q_far, kvs)
    theirs = swap_core(for_other)
    top = jnp.maximum(mine[0], theirs[0])
    mine_by, theirs_by = jnp.exp2(mine[0] - top), jnp.exp2(theirs[0] - top)
    both = jnp.stack([top, mine[1] * mine_by + theirs[1] * theirs_by, mine[2] * mine_by + theirs[2] * theirs_by])
    stats = [both] + [back(both, "y", k) for k in (1, 2, 3)]

    common = (span_order, stats, q_near, q_far, kvs)
    (dkv1, dkv2, dkv3), (dqt,) = call_grads((1, 2, 3), True, False, *common, None)
    (dkv0,), (dq_keep, dq_send) = call_grads((0,), False, True, *common, dqt)
    z1, z2, z3 = ahead(dkv1, "z", 1), ahead(dkv2, "z", 2), ahead(dkv3, "z", 3)
    (summed,) = plain_call(middle_kernel, "middle", [((PIECE, DH), BF16)], dkv0, z1, z2, z3)
    dq_send, summed = lax.optimization_barrier((dq_send, summed))
    dq_other = swap_core(dq_send)
    rows = (2 * SPAN, DH)
    dq, r1, r2, r3 = plain_call(
        query_kernel, "query", [(rows, F32), (rows, BF16), (rows, BF16), (rows, BF16)], dq_keep, dq_other
    )
    xs = [back(summed, "x", k) for k in (1, 2, 3)]
    ys = [ahead(part, "y", k) for k, part in ((1, r1), (2, r2), (3, r3))]
    return plain_call(last_kernel, "last", [(rows, BF16)] * 3, summed, *xs, dq, *ys)


def solution(mesh):
    fine = Mesh(mesh.devices.reshape(4, 4, 2, 4), ("z", "y", "c", "x"))
    ctx = ("z", "y", "c")
    return jax.shard_map(
        local,
        mesh=fine,
        in_specs=(P(), P(ctx, "x"), P(ctx, None), P(ctx, None), P(ctx, "x")),
        out_specs=(P(ctx, "x"), P(ctx, None), P(ctx, None)),
        check_vma=False,
    )
```

```python
import functools

import jax
import jax.numpy as jnp
from jax import lax
from jax.experimental import pallas as pl
from jax.experimental.pallas import tpu as pltpu
from jax.sharding import Mesh, PartitionSpec as P

DH = 128
SPAN = 256
SCALE = DH ** (-0.5)
LOG2E = 1.4426950408889634
SCALE2 = SCALE * LOG2E
NEG = -1e30
NT = (((1,), (1,)), ((), ()))
NN = (((1,), (0,)), ((), ()))
F32 = jnp.float32
BF16 = jnp.bfloat16


def spans_of(order_ref, z, y, c):
    row = (z * 4 + y) * 2 + c
    first, second = order_ref[row, 0], order_ref[row, 1]
    return jnp.minimum(first, second), jnp.where(first < second, 0, 1)


def query_spans(order_ref, a):
    z, y, c = lax.axis_index("z"), lax.axis_index("y"), lax.axis_index("c")
    return spans_of(order_ref, z, (y + 4 - a % 4) % 4, (c + a // 4) % 2)


def key_spans(order_ref, b):
    z, y, c = lax.axis_index("z"), lax.axis_index("y"), lax.axis_index("c")
    return spans_of(order_ref, (z + 4 - b) % 4, y, c)


def one_query_piece(order_ref, tile, a, pieces, own):
    low, low_slot = query_spans(order_ref, a)
    found = [key_spans(order_ref, b) for b in pieces]
    tile(a, 1 - low_slot, [(b, slot) for b, (_, slot) in zip(pieces, found)], False)
    for b, (key_low, key_slot) in zip(pieces, found):
        if own and b == 0:
            tile(0, 0, [(0, 0)], True)
            tile(0, 1, [(0, 1)], True)
        else:
            lows = low > key_low
            tile(a, jnp.where(lows, low_slot, 1 - low_slot), [(b, jnp.where(lows, key_slot, 1 - key_slot))], False)


def half(ref, piece, which, second):
    begin = which * SPAN + second * 2 * SPAN
    if not isinstance(begin, int):
        begin = pl.multiple_of(begin, SPAN)
    return ref[piece, pl.ds(begin, SPAN), :]


def products(q_ref, kv_ref, a, q_which, b, k_which):
    scores = lax.dot_general(
        half(kv_ref, b, k_which, 0), half(q_ref, a, q_which, 0), NT, preferred_element_type=F32
    )
    dprobs = lax.dot_general(
        half(kv_ref, b, k_which, 1), half(q_ref, a, q_which, 1), NT, preferred_element_type=F32
    )
    return scores * SCALE2, dprobs


def diagonal_visible():
    key_row = lax.broadcasted_iota(jnp.int32, (SPAN, SPAN), 0)
    query_row = lax.broadcasted_iota(jnp.int32, (SPAN, SPAN), 1)
    return key_row <= query_row


def query_place(a):
    y, c = lax.axis_index("y"), lax.axis_index("c")
    return 2 * (((y + 4 - a % 4) % 4) * 2 + (c + a // 4) % 2)


def in_flight(begin, finish, depth):
    waiting = []

    def tile(a, q_which, keys, masked):
        for b, k_which in keys:
            waiting.append(begin(a, q_which, b, k_which, masked))
            if len(waiting) > depth:
                finish(waiting.pop(0))

    def drain():
        while waiting:
            finish(waiting.pop(0))

    return tile, drain


def run_tiles(order_ref, tile, drain, pieces):
    start, step = 0, max(2, 4 // len(pieces))
    if 0 in pieces:
        one_query_piece(order_ref, tile, 0, pieces, True)
        one_query_piece(order_ref, tile, 1, pieces, False)
        start, step = 2, 3 if len(pieces) == 1 else 2
        drain()

    def some(i, carry):
        for j in range(step):
            one_query_piece(order_ref, tile, start + i * step + j, pieces, False)
        drain()
        return carry

    lax.fori_loop(0, (8 - start) // step, some, 0)


def stats_kernel(pieces, first, last, *refs):
    refs = list(refs)
    order_ref, near_ref, far_ref = refs[:3]
    del refs[:3]
    kv_refs = refs[: len(pieces)]
    del refs[: len(pieces)]
    before = [] if first else refs[:3]
    del refs[: len(before)]
    if last:
        out_ref = refs.pop(0)
        q_ref, kv_ref, top_ref, total_ref, weighted_ref = refs
    else:
        top_ref, total_ref, weighted_ref, q_ref, kv_ref = refs
    q_ref[0:4] = near_ref[...].reshape(4, PIECE, DH)
    q_ref[4:8] = far_ref[...].reshape(4, PIECE, DH)
    for i, ref in enumerate(kv_refs):
        kv_ref[i] = ref[...]
    if first:
        top_ref[...] = jnp.full(top_ref.shape, NEG, F32)
        total_ref[...] = jnp.zeros(total_ref.shape, F32)
        weighted_ref[...] = jnp.zeros(weighted_ref.shape, F32)
    else:
        for ref, source in zip((top_ref, total_ref, weighted_ref), before):
            ref[...] = source[...]

    def begin(a, q_which, b, k_which, masked):
        scores, dprobs = products(q_ref, kv_ref, a, q_which, pieces.index(b), k_which)
        if masked:
            scores = jnp.where(diagonal_visible(), scores, NEG)
        return a * 2 + q_which, masked, scores.reshape(32, 8, SPAN), dprobs.reshape(32, 8, SPAN)

    def finish(state):
        slot, masked, scores, dprobs = state
        old = top_ref[slot]
        top = jnp.maximum(old, jnp.max(scores, axis=0))
        shrink = jnp.exp2(old - top)
        expon = jnp.exp2(scores - top[None])
        if masked:
            expon = jnp.where(diagonal_visible().reshape(32, 8, SPAN), expon, 0.0)
        top_ref[slot] = top
        total_ref[slot] = total_ref[slot] * shrink + jnp.sum(expon, axis=0)
        weighted_ref[slot] = weighted_ref[slot] * shrink + jnp.sum(expon * dprobs, axis=0)

    run_tiles(order_ref, *in_flight(begin, finish, 2), pieces)
    if not last:
        return
    for slot in range(16):
        tops = top_ref[slot]
        top = jnp.max(tops, axis=0, keepdims=True)
        factor = jnp.exp2(tops - top)
        rows = (
            top,
            jnp.sum(total_ref[slot] * factor, axis=0, keepdims=True),
            jnp.sum(weighted_ref[slot] * factor, axis=0, keepdims=True),
        )
        place = query_place(slot // 2) + slot % 2
        for kind, row in enumerate(rows):
            out_ref[kind, pl.ds(place, 1), :] = row


def norm_and_delta(stat_refs, sum_ref, norm_ref, delta_ref):
    found = [[ref[kind] for kind in range(3)] for ref in stat_refs]
    top = functools.reduce(jnp.maximum, [f[0] for f in found])
    factors = [jnp.exp2(f[0] - top) for f in found]
    total = sum(f[1] * g for f, g in zip(found, factors))
    sum_ref[0] = top + jnp.log2(total)
    sum_ref[1] = sum(f[2] * g for f, g in zip(found, factors)) / total
    for slot in range(16):
        place = query_place(slot // 2) + slot % 2
        norm_ref[slot] = jnp.broadcast_to(sum_ref[0, pl.ds(place, 1), :], (8, SPAN))
        delta_ref[slot] = jnp.broadcast_to(sum_ref[1, pl.ds(place, 1), :], (8, SPAN))


def grads_kernel(pieces, first, last, *refs):
    refs = list(refs)
    order_ref, stat_refs, near_ref, far_ref = refs[0], refs[1:5], refs[5], refs[6]
    del refs[:7]
    kv_refs = refs[: len(pieces)]
    del refs[: len(pieces)]
    dqt_in = None if first else refs.pop(0)
    dkv_refs = dict(zip(pieces, refs[: len(pieces)]))
    del refs[: len(pieces)]
    dq_outs = [refs.pop(0), refs.pop(0)] if last else [refs.pop(0)]
    q_ref, kv_ref, sum_ref, norm_ref, delta_ref, dk_ref, dv_ref, kt_ref = refs[:8]
    dqt_ref = refs[8] if last else dq_outs[0]

    norm_and_delta(stat_refs, sum_ref, norm_ref, delta_ref)
    q_ref[0:4] = near_ref[...].reshape(4, PIECE, DH)
    q_ref[4:8] = far_ref[...].reshape(4, PIECE, DH)
    for i, b in enumerate(pieces):
        kv_ref[i] = kv_refs[i][...]
        for which in range(2):
            kt_ref[2 * i + which] = kv_ref[i, pl.ds(which * SPAN, SPAN), :].T
    dk_ref[...] = jnp.zeros(dk_ref.shape, F32)
    dv_ref[...] = jnp.zeros(dv_ref.shape, F32)
    if first:
        dqt_ref[...] = jnp.zeros(dqt_ref.shape, F32)
    else:
        dqt_ref[...] = dqt_in[...]

    def begin(a, q_which, b, k_which, masked):
        slot = a * 2 + q_which
        queries = half(q_ref, a, q_which, 0)
        out_grads = half(q_ref, a, q_which, 1)
        i = pieces.index(b)
        scores = lax.dot_general(
            half(kv_ref, i, k_which, 0), queries, NT, preferred_element_type=F32
        ) * SCALE2
        dprobs = lax.dot_general(
            half(kv_ref, i, k_which, 1), out_grads, NT, preferred_element_type=F32
        )
        return slot, 2 * i + k_which, masked, queries, out_grads, scores, dprobs

    def finish(state):
        slot, key_slot, masked, queries, out_grads, scores, dprobs = state
        probs = jnp.exp2(scores.reshape(32, 8, SPAN) - norm_ref[slot][None])
        if masked:
            probs = jnp.where(diagonal_visible().reshape(32, 8, SPAN), probs, 0.0)
        dscores = probs * (dprobs.reshape(32, 8, SPAN) - delta_ref[slot][None])
        probs = probs.reshape(SPAN, SPAN).astype(BF16)
        dscores = dscores.reshape(SPAN, SPAN).astype(BF16)
        dv_ref[key_slot] += lax.dot_general(probs, out_grads, NN, preferred_element_type=F32)
        dk_ref[key_slot] += lax.dot_general(dscores, queries, NN, preferred_element_type=F32)
        dqt_ref[slot] += lax.dot_general(kt_ref[key_slot], dscores, NN, preferred_element_type=F32)

    run_tiles(order_ref, *in_flight(begin, finish, 1), pieces)
    for i, b in enumerate(pieces):
        ref = dkv_refs[b]
        for which in range(2):
            ref[pl.ds(which * SPAN, SPAN), :] = dk_ref[2 * i + which].astype(ref.dtype)
            ref[pl.ds((2 + which) * SPAN, SPAN), :] = dv_ref[2 * i + which].astype(ref.dtype)
    if last:
        for out, begin in zip(dq_outs, (0, 8)):
            for slot in range(8):
                out[pl.ds(slot * SPAN, SPAN), :] = dqt_ref[begin + slot].T.astype(out.dtype)


def pack_kernel(queries_ref, keys_ref, values_ref, grads_ref, q_ref, kv_ref, sems):
    rows = 2 * SPAN
    copies = []
    for i, (source, target) in enumerate(
        ((queries_ref, q_ref), (grads_ref, q_ref), (keys_ref, kv_ref), (values_ref, kv_ref))
    ):
        place = target.at[pl.ds((i % 2) * rows, rows), :]
        copies.append(pltpu.make_async_copy(source, place, sems.at[i]))
    for copy in copies:
        copy.start()
    for copy in copies:
        copy.wait()


def middle_kernel(dkv_ref, z1_ref, z2_ref, z3_ref, sum_ref):
    total = dkv_ref[...] + z1_ref[...].astype(F32) + z2_ref[...].astype(F32) + z3_ref[...].astype(F32)
    sum_ref[...] = total.astype(BF16)


def query_kernel(keep_ref, other_ref, dq_ref, r1_ref, r2_ref, r3_ref):
    for k, ref in enumerate((dq_ref, r1_ref, r2_ref, r3_ref)):
        rows = pl.ds(k * 2 * SPAN, 2 * SPAN)
        ref[...] = (keep_ref[rows, :] + other_ref[rows, :].astype(F32)).astype(ref.dtype)


def last_kernel(sum_ref, x1_ref, x2_ref, x3_ref, dq_ref, y1_ref, y2_ref, y3_ref, q_out, k_out, v_out):
    own, x1, x2, x3 = [ref[...].astype(F32) for ref in (sum_ref, x1_ref, x2_ref, x3_ref)]
    total = (own + x2) + (x1 + x3)
    k_out[...] = (total[: 2 * SPAN] * SCALE).astype(BF16)
    v_out[...] = total[2 * SPAN :].astype(BF16)
    dq = dq_ref[...]
    for ref in (y1_ref, y2_ref, y3_ref):
        dq = dq + ref[...].astype(F32)
    q_out[...] = (dq * SCALE).astype(BF16)


SMEM = pl.BlockSpec(memory_space=pltpu.SMEM)
VMEM = pl.BlockSpec(memory_space=pltpu.VMEM)
PIECE = 4 * SPAN


def call_stats(pieces, first, last, span_order, q_near, q_far, kvs, before):
    shape = (3, 16, SPAN) if last else (16, 8, SPAN)
    running = [pltpu.VMEM((16, 8, SPAN), F32)] * 3 if last else []
    args = [span_order, q_near, q_far, *[kvs[b] for b in pieces], *before]
    return pl.pallas_call(
        functools.partial(stats_kernel, pieces, first, last),
        out_shape=(jax.ShapeDtypeStruct(shape, F32),) * (1 if last else 3),
        in_specs=[SMEM] + [VMEM] * (len(args) - 1),
        out_specs=(VMEM,) * (1 if last else 3),
        scratch_shapes=[pltpu.VMEM((8, PIECE, DH), BF16), pltpu.VMEM((len(pieces), PIECE, DH), BF16)] + running,
        compiler_params=pltpu.CompilerParams(vmem_limit_bytes=32 * 2**20),
        cost_estimate=pl.CostEstimate(
            flops=16 * len(pieces) * 2 * 2 * SPAN * SPAN * DH,
            bytes_accessed=3 * 2**20,
            transcendentals=16 * len(pieces) * SPAN * SPAN,
        ),
        name="stats",
    )(*args)


def call_grads(pieces, first, last, span_order, stats, q_near, q_far, kvs, dqt):
    tiles = 16 * len(pieces)
    dkv_shapes = tuple(jax.ShapeDtypeStruct((PIECE, DH), BF16 if b else F32) for b in pieces)
    if last:
        dq_shapes = tuple(jax.ShapeDtypeStruct((8 * SPAN, DH), dtype) for dtype in (F32, BF16))
    else:
        dq_shapes = (jax.ShapeDtypeStruct((16, DH, SPAN), F32),)
    args = [span_order, *stats, q_near, q_far, *[kvs[b] for b in pieces]] + ([] if first else [dqt])
    out = pl.pallas_call(
        functools.partial(grads_kernel, pieces, first, last),
        out_shape=dkv_shapes + dq_shapes,
        in_specs=[SMEM] + [VMEM] * (len(args) - 1),
        out_specs=(VMEM,) * (len(pieces) + len(dq_shapes)),
        scratch_shapes=[
            pltpu.VMEM((8, PIECE, DH), BF16),
            pltpu.VMEM((len(pieces), PIECE, DH), BF16),
            pltpu.VMEM((2, 16, SPAN), F32),
            pltpu.VMEM((16, 8, SPAN), F32),
            pltpu.VMEM((16, 8, SPAN), F32),
            pltpu.VMEM((2 * len(pieces), SPAN, DH), F32),
            pltpu.VMEM((2 * len(pieces), SPAN, DH), F32),
            pltpu.VMEM((2 * len(pieces), DH, SPAN), BF16),
        ]
        + ([pltpu.VMEM((16, DH, SPAN), F32)] if last else []),
        compiler_params=pltpu.CompilerParams(vmem_limit_bytes=32 * 2**20),
        cost_estimate=pl.CostEstimate(
            flops=tiles * 5 * 2 * SPAN * SPAN * DH, bytes_accessed=4 * 2**20, transcendentals=tiles * SPAN * SPAN
        ),
        name="grads",
    )(*args)
    return out[: len(pieces)], out[len(pieces) :]


def plain_call(kernel, name, out_shapes, *args):
    return pl.pallas_call(
        kernel,
        out_shape=tuple(jax.ShapeDtypeStruct(shape, dtype) for shape, dtype in out_shapes),
        in_specs=[VMEM] * len(args),
        out_specs=(VMEM,) * len(out_shapes),
        compiler_params=pltpu.CompilerParams(vmem_limit_bytes=16 * 2**20),
        cost_estimate=pl.CostEstimate(flops=2**20, bytes_accessed=2**21, transcendentals=0),
        name=name,
    )(*args)


def call_pack(*args):
    return pl.pallas_call(
        pack_kernel,
        out_shape=(jax.ShapeDtypeStruct((PIECE, DH), BF16),) * 2,
        in_specs=[pl.BlockSpec(memory_space=pl.ANY)] * 4,
        out_specs=(VMEM, VMEM),
        scratch_shapes=[pltpu.SemaphoreType.DMA((4,))],
        compiler_params=pltpu.CompilerParams(vmem_limit_bytes=56 * 2**20),
        name="pack",
    )(*args)


def back(value, axis, k):
    return lax.ppermute(value, axis, [(i, (i + k) % 4) for i in range(4)])


def ahead(value, axis, k):
    return lax.ppermute(value, axis, [(i, (i - k) % 4) for i in range(4)])


def swap_core(value):
    return lax.ppermute(value, "c", [(0, 1), (1, 0)])


def merged(mine, theirs):
    top = jnp.maximum(mine[0], theirs[0])
    mine_by, theirs_by = jnp.exp2(mine[0] - top), jnp.exp2(theirs[0] - top)
    return jnp.stack([top, mine[1] * mine_by + theirs[1] * theirs_by, mine[2] * mine_by + theirs[2] * theirs_by])


def local(span_order, queries, key_rows, value_rows, out_grads):
    q_own, kv_own = call_pack(queries, key_rows, value_rows, out_grads)
    q_got = [back(q_own, "y", k) for k in (1, 2, 3)]
    kv_got = [back(kv_own, "z", k) for k in (1, 2, 3)]
    q_got, kv_got[0], kv_got[2] = lax.optimization_barrier((q_got, kv_got[0], kv_got[2]))
    q_near = jnp.concatenate([q_own] + q_got, axis=0)
    q_far = swap_core(q_near)
    kvs = [kv_own] + kv_got

    running = call_stats((0, 1, 3), True, False, span_order, q_near, q_far, kvs, ())
    (stats,) = call_stats((2,), False, True, span_order, q_near, q_far, kvs, running)
    stats = merged(stats, swap_core(stats))
    stats = [stats] + [back(stats, "y", k) for k in (1, 2, 3)]

    common = (span_order, stats, q_near, q_far, kvs)
    (dkv1, dkv2, dkv3), (dqt,) = call_grads((1, 2, 3), True, False, *common, None)
    (dkv0,), (dq_keep, dq_send) = call_grads((0,), False, True, *common, dqt)
    z1, z2, z3 = ahead(dkv1, "z", 1), ahead(dkv2, "z", 2), ahead(dkv3, "z", 3)
    (summed,) = plain_call(middle_kernel, "middle", [((PIECE, DH), BF16)], dkv0, z1, z2, z3)
    dq_send, summed = lax.optimization_barrier((dq_send, summed))
    dq_other = swap_core(dq_send)
    rows = (2 * SPAN, DH)
    dq, r1, r2, r3 = plain_call(
        query_kernel, "query", [(rows, F32), (rows, BF16), (rows, BF16), (rows, BF16)], dq_keep, dq_other
    )
    xs = [back(summed, "x", k) for k in (1, 2, 3)]
    ys = [ahead(part, "y", k) for k, part in ((1, r1), (2, r2), (3, r3))]
    return plain_call(last_kernel, "last", [(rows, BF16)] * 3, summed, *xs, dq, *ys)


def solution(mesh):
    fine = Mesh(mesh.devices.reshape(4, 4, 2, 4), ("z", "y", "c", "x"))
    ctx = ("z", "y", "c")
    return jax.shard_map(
        local,
        mesh=fine,
        in_specs=(P(), P(ctx, "x"), P(ctx, None), P(ctx, None), P(ctx, "x")),
        out_specs=(P(ctx, "x"), P(ctx, None), P(ctx, None)),
        check_vma=False,
    )
```

```python
import functools

import jax
import jax.numpy as jnp
from jax import lax
from jax.experimental import pallas as pl
from jax.experimental.pallas import tpu as pltpu
from jax.sharding import Mesh, PartitionSpec as P

DH = 128
SPAN = 256
SCALE = DH ** (-0.5)
LOG2E = 1.4426950408889634
SCALE2 = SCALE * LOG2E
NEG = -1e30
NT = (((1,), (1,)), ((), ()))
NN = (((1,), (0,)), ((), ()))
F32 = jnp.float32
BF16 = jnp.bfloat16


def spans_of(order_ref, z, y, c):
    row = (z * 4 + y) * 2 + c
    first, second = order_ref[row, 0], order_ref[row, 1]
    return jnp.minimum(first, second), jnp.where(first < second, 0, 1)


def query_spans(order_ref, a):
    z, y, c = lax.axis_index("z"), lax.axis_index("y"), lax.axis_index("c")
    return spans_of(order_ref, z, (y + 4 - a % 4) % 4, (c + a // 4) % 2)


def key_spans(order_ref, b):
    z, y, c = lax.axis_index("z"), lax.axis_index("y"), lax.axis_index("c")
    return spans_of(order_ref, (z + 4 - b) % 4, y, c)


def one_query_piece(order_ref, tile, a, pieces, own):
    low, low_slot = query_spans(order_ref, a)
    found = [key_spans(order_ref, b) for b in pieces]
    tile(a, 1 - low_slot, [(b, slot) for b, (_, slot) in zip(pieces, found)], False)
    for b, (key_low, key_slot) in zip(pieces, found):
        if own and b == 0:
            tile(0, 0, [(0, 0)], True)
            tile(0, 1, [(0, 1)], True)
        else:
            lows = low > key_low
            tile(a, jnp.where(lows, low_slot, 1 - low_slot), [(b, jnp.where(lows, key_slot, 1 - key_slot))], False)


def half(ref, piece, which, second):
    begin = which * SPAN + second * 2 * SPAN
    if not isinstance(begin, int):
        begin = pl.multiple_of(begin, SPAN)
    return ref[piece, pl.ds(begin, SPAN), :]


def products(q_ref, kv_ref, a, q_which, b, k_which):
    scores = lax.dot_general(
        half(kv_ref, b, k_which, 0), half(q_ref, a, q_which, 0), NT, preferred_element_type=F32
    )
    dprobs = lax.dot_general(
        half(kv_ref, b, k_which, 1), half(q_ref, a, q_which, 1), NT, preferred_element_type=F32
    )
    return scores * SCALE2, dprobs


def diagonal_visible():
    key_row = lax.broadcasted_iota(jnp.int32, (SPAN, SPAN), 0)
    query_row = lax.broadcasted_iota(jnp.int32, (SPAN, SPAN), 1)
    return key_row <= query_row


def query_place(a):
    y, c = lax.axis_index("y"), lax.axis_index("c")
    return 2 * (((y + 4 - a % 4) % 4) * 2 + (c + a // 4) % 2)


def in_flight(begin, finish, depth):
    waiting = []

    def tile(a, q_which, keys, masked):
        for b, k_which in keys:
            waiting.append(begin(a, q_which, b, k_which, masked))
            if len(waiting) > depth:
                finish(waiting.pop(0))

    def drain():
        while waiting:
            finish(waiting.pop(0))

    return tile, drain


def run_tiles(order_ref, tile, drain, pieces):
    start, step = 0, max(2, 4 // len(pieces))
    if 0 in pieces:
        one_query_piece(order_ref, tile, 0, pieces, True)
        one_query_piece(order_ref, tile, 1, pieces, False)
        start, step = 2, 3 if len(pieces) == 1 else 2
        drain()

    def some(i, carry):
        for j in range(step):
            one_query_piece(order_ref, tile, start + i * step + j, pieces, False)
        drain()
        return carry

    lax.fori_loop(0, (8 - start) // step, some, 0)


def stats_kernel(far, order_ref, q_ref, *refs):
    kv_refs, refs = refs[:4], refs[4:]
    if far:
        before_ref, refs = refs[0], refs[1:]
    out_ref, kv_ref, top_ref, total_ref, weighted_ref = refs
    if far:
        out_ref[...] = before_ref[...]
    for b, ref in enumerate(kv_refs):
        kv_ref[b] = ref[...]
    top_ref[...] = jnp.full(top_ref.shape, NEG, F32)
    total_ref[...] = jnp.zeros(total_ref.shape, F32)
    weighted_ref[...] = jnp.zeros(weighted_ref.shape, F32)
    base = 4 if far else 0
    pieces = (0, 1, 2, 3)

    def begin(a, q_which, b, k_which, masked):
        scores, dprobs = products(q_ref, kv_ref, a - base, q_which, b, k_which)
        if masked:
            scores = jnp.where(diagonal_visible(), scores, NEG)
        return (a - base) * 2 + q_which, masked, scores.reshape(32, 8, SPAN), dprobs.reshape(32, 8, SPAN)

    def finish(state):
        slot, masked, scores, dprobs = state
        old = top_ref[slot]
        top = jnp.maximum(old, jnp.max(scores, axis=0))
        shrink = jnp.exp2(old - top)
        expon = jnp.exp2(scores - top[None])
        if masked:
            expon = jnp.where(diagonal_visible().reshape(32, 8, SPAN), expon, 0.0)
        top_ref[slot] = top
        total_ref[slot] = total_ref[slot] * shrink + jnp.sum(expon, axis=0)
        weighted_ref[slot] = weighted_ref[slot] * shrink + jnp.sum(expon * dprobs, axis=0)

    tile, drain = in_flight(begin, finish, 2)
    step = 2 if far else 1
    if not far:
        one_query_piece(order_ref, tile, 0, pieces, True)
        drain()

    def some(i, carry):
        for j in range(step):
            one_query_piece(order_ref, tile, (4 if far else 1) + i * step + j, pieces, False)
        drain()
        return carry

    lax.fori_loop(0, 2 if far else 3, some, 0)
    for slot in range(8):
        tops = top_ref[slot]
        top = jnp.max(tops, axis=0, keepdims=True)
        factor = jnp.exp2(tops - top)
        rows = (
            top,
            jnp.sum(total_ref[slot] * factor, axis=0, keepdims=True),
            jnp.sum(weighted_ref[slot] * factor, axis=0, keepdims=True),
        )
        place = query_place(base + slot // 2) + slot % 2
        for kind, row in enumerate(rows):
            out_ref[kind, pl.ds(place, 1), :] = row


def norm_and_delta(stat_refs, sum_ref, norm_ref, delta_ref):
    found = [[ref[kind] for kind in range(3)] for ref in stat_refs]
    top = functools.reduce(jnp.maximum, [f[0] for f in found])
    factors = [jnp.exp2(f[0] - top) for f in found]
    total = sum(f[1] * g for f, g in zip(found, factors))
    sum_ref[0] = top + jnp.log2(total)
    sum_ref[1] = sum(f[2] * g for f, g in zip(found, factors)) / total
    for slot in range(16):
        place = query_place(slot // 2) + slot % 2
        norm_ref[slot] = jnp.broadcast_to(sum_ref[0, pl.ds(place, 1), :], (8, SPAN))
        delta_ref[slot] = jnp.broadcast_to(sum_ref[1, pl.ds(place, 1), :], (8, SPAN))


def grads_kernel(pieces, first, last, *refs):
    refs = list(refs)
    order_ref, stat_refs, near_ref, far_ref = refs[0], refs[1:5], refs[5], refs[6]
    del refs[:7]
    kv_refs = refs[: len(pieces)]
    del refs[: len(pieces)]
    dqt_in = None if first else refs.pop(0)
    dkv_refs = dict(zip(pieces, refs[: len(pieces)]))
    del refs[: len(pieces)]
    dq_outs = [refs.pop(0), refs.pop(0)] if last else [refs.pop(0)]
    q_ref, kv_ref, sum_ref, norm_ref, delta_ref, dk_ref, dv_ref, kt_ref = refs[:8]
    dqt_ref = refs[8] if last else dq_outs[0]

    norm_and_delta(stat_refs, sum_ref, norm_ref, delta_ref)
    q_ref[0:4] = near_ref[...].reshape(4, PIECE, DH)
    q_ref[4:8] = far_ref[...].reshape(4, PIECE, DH)
    for i, b in enumerate(pieces):
        kv_ref[i] = kv_refs[i][...]
        for which in range(2):
            kt_ref[2 * i + which] = kv_ref[i, pl.ds(which * SPAN, SPAN), :].T
    dk_ref[...] = jnp.zeros(dk_ref.shape, F32)
    dv_ref[...] = jnp.zeros(dv_ref.shape, F32)
    if first:
        dqt_ref[...] = jnp.zeros(dqt_ref.shape, F32)
    else:
        dqt_ref[...] = dqt_in[...]

    def begin(a, q_which, b, k_which, masked):
        slot = a * 2 + q_which
        queries = half(q_ref, a, q_which, 0)
        out_grads = half(q_ref, a, q_which, 1)
        i = pieces.index(b)
        scores = lax.dot_general(
            half(kv_ref, i, k_which, 0), queries, NT, preferred_element_type=F32
        ) * SCALE2
        dprobs = lax.dot_general(
            half(kv_ref, i, k_which, 1), out_grads, NT, preferred_element_type=F32
        )
        return slot, 2 * i + k_which, masked, queries, out_grads, scores, dprobs

    def finish(state):
        slot, key_slot, masked, queries, out_grads, scores, dprobs = state
        probs = jnp.exp2(scores.reshape(32, 8, SPAN) - norm_ref[slot][None])
        if masked:
            probs = jnp.where(diagonal_visible().reshape(32, 8, SPAN), probs, 0.0)
        dscores = probs * (dprobs.reshape(32, 8, SPAN) - delta_ref[slot][None])
        probs = probs.reshape(SPAN, SPAN).astype(BF16)
        dscores = dscores.reshape(SPAN, SPAN).astype(BF16)
        dv_ref[key_slot] += lax.dot_general(probs, out_grads, NN, preferred_element_type=F32)
        dk_ref[key_slot] += lax.dot_general(dscores, queries, NN, preferred_element_type=F32)
        dqt_ref[slot] += lax.dot_general(kt_ref[key_slot], dscores, NN, preferred_element_type=F32)

    run_tiles(order_ref, *in_flight(begin, finish, 1), pieces)
    for i, b in enumerate(pieces):
        ref = dkv_refs[b]
        for which in range(2):
            ref[pl.ds(which * SPAN, SPAN), :] = dk_ref[2 * i + which].astype(ref.dtype)
            ref[pl.ds((2 + which) * SPAN, SPAN), :] = dv_ref[2 * i + which].astype(ref.dtype)
    if last:
        for out, begin in zip(dq_outs, (0, 8)):
            for slot in range(8):
                out[pl.ds(slot * SPAN, SPAN), :] = dqt_ref[begin + slot].T.astype(out.dtype)


def pack_kernel(queries_ref, keys_ref, values_ref, grads_ref, q_ref, kv_ref, sems):
    rows = 2 * SPAN
    copies = []
    for i, (source, target) in enumerate(
        ((queries_ref, q_ref), (grads_ref, q_ref), (keys_ref, kv_ref), (values_ref, kv_ref))
    ):
        place = target.at[pl.ds((i % 2) * rows, rows), :]
        copies.append(pltpu.make_async_copy(source, place, sems.at[i]))
    for copy in copies:
        copy.start()
    for copy in copies:
        copy.wait()


def middle_kernel(dkv_ref, z1_ref, z2_ref, z3_ref, sum_ref):
    total = dkv_ref[...] + z1_ref[...].astype(F32) + z2_ref[...].astype(F32) + z3_ref[...].astype(F32)
    sum_ref[...] = total.astype(BF16)


def query_kernel(keep_ref, other_ref, dq_ref, r1_ref, r2_ref, r3_ref):
    for k, ref in enumerate((dq_ref, r1_ref, r2_ref, r3_ref)):
        rows = pl.ds(k * 2 * SPAN, 2 * SPAN)
        ref[...] = (keep_ref[rows, :] + other_ref[rows, :].astype(F32)).astype(ref.dtype)


def last_kernel(sum_ref, x1_ref, x2_ref, x3_ref, dq_ref, y1_ref, y2_ref, y3_ref, q_out, k_out, v_out):
    own, x1, x2, x3 = [ref[...].astype(F32) for ref in (sum_ref, x1_ref, x2_ref, x3_ref)]
    total = (own + x2) + (x1 + x3)
    k_out[...] = (total[: 2 * SPAN] * SCALE).astype(BF16)
    v_out[...] = total[2 * SPAN :].astype(BF16)
    dq = dq_ref[...]
    for ref in (y1_ref, y2_ref, y3_ref):
        dq = dq + ref[...].astype(F32)
    q_out[...] = (dq * SCALE).astype(BF16)


SMEM = pl.BlockSpec(memory_space=pltpu.SMEM)
VMEM = pl.BlockSpec(memory_space=pltpu.VMEM)
PIECE = 4 * SPAN


def call_stats(far, span_order, q_pieces, kvs, *before):
    args = [span_order, q_pieces.reshape(4, PIECE, DH), *kvs, *before]
    return pl.pallas_call(
        functools.partial(stats_kernel, far),
        out_shape=jax.ShapeDtypeStruct((3, 16, SPAN), F32),
        in_specs=[SMEM] + [VMEM] * (len(args) - 1),
        out_specs=VMEM,
        scratch_shapes=[pltpu.VMEM((4, PIECE, DH), BF16)] + [pltpu.VMEM((8, 8, SPAN), F32)] * 3,
        compiler_params=pltpu.CompilerParams(vmem_limit_bytes=32 * 2**20),
        cost_estimate=pl.CostEstimate(
            flops=32 * 2 * 2 * SPAN * SPAN * DH, bytes_accessed=2**21, transcendentals=32 * SPAN * SPAN
        ),
        name="stats",
    )(*args)


def call_grads(pieces, first, last, span_order, stats, q_near, q_far, kvs, dqt):
    tiles = 16 * len(pieces)
    dkv_shapes = tuple(jax.ShapeDtypeStruct((PIECE, DH), BF16 if b else F32) for b in pieces)
    if last:
        dq_shapes = tuple(jax.ShapeDtypeStruct((8 * SPAN, DH), dtype) for dtype in (F32, BF16))
    else:
        dq_shapes = (jax.ShapeDtypeStruct((16, DH, SPAN), F32),)
    args = [span_order, *stats, q_near, q_far, *[kvs[b] for b in pieces]] + ([] if first else [dqt])
    out = pl.pallas_call(
        functools.partial(grads_kernel, pieces, first, last),
        out_shape=dkv_shapes + dq_shapes,
        in_specs=[SMEM] + [VMEM] * (len(args) - 1),
        out_specs=(VMEM,) * (len(pieces) + len(dq_shapes)),
        scratch_shapes=[
            pltpu.VMEM((8, PIECE, DH), BF16),
            pltpu.VMEM((len(pieces), PIECE, DH), BF16),
            pltpu.VMEM((2, 16, SPAN), F32),
            pltpu.VMEM((16, 8, SPAN), F32),
            pltpu.VMEM((16, 8, SPAN), F32),
            pltpu.VMEM((2 * len(pieces), SPAN, DH), F32),
            pltpu.VMEM((2 * len(pieces), SPAN, DH), F32),
            pltpu.VMEM((2 * len(pieces), DH, SPAN), BF16),
        ]
        + ([pltpu.VMEM((16, DH, SPAN), F32)] if last else []),
        compiler_params=pltpu.CompilerParams(vmem_limit_bytes=32 * 2**20),
        cost_estimate=pl.CostEstimate(
            flops=tiles * 5 * 2 * SPAN * SPAN * DH, bytes_accessed=4 * 2**20, transcendentals=tiles * SPAN * SPAN
        ),
        name="grads",
    )(*args)
    return out[: len(pieces)], out[len(pieces) :]


def plain_call(kernel, name, out_shapes, *args):
    return pl.pallas_call(
        kernel,
        out_shape=tuple(jax.ShapeDtypeStruct(shape, dtype) for shape, dtype in out_shapes),
        in_specs=[VMEM] * len(args),
        out_specs=(VMEM,) * len(out_shapes),
        compiler_params=pltpu.CompilerParams(vmem_limit_bytes=16 * 2**20),
        cost_estimate=pl.CostEstimate(flops=2**20, bytes_accessed=2**21, transcendentals=0),
        name=name,
    )(*args)


def call_pack(*args):
    return pl.pallas_call(
        pack_kernel,
        out_shape=(jax.ShapeDtypeStruct((PIECE, DH), BF16),) * 2,
        in_specs=[pl.BlockSpec(memory_space=pl.ANY)] * 4,
        out_specs=(VMEM, VMEM),
        scratch_shapes=[pltpu.SemaphoreType.DMA((4,))],
        compiler_params=pltpu.CompilerParams(vmem_limit_bytes=56 * 2**20),
        name="pack",
    )(*args)


def back(value, axis, k):
    return lax.ppermute(value, axis, [(i, (i + k) % 4) for i in range(4)])


def ahead(value, axis, k):
    return lax.ppermute(value, axis, [(i, (i - k) % 4) for i in range(4)])


def swap_core(value):
    return lax.ppermute(value, "c", [(0, 1), (1, 0)])


def merged(mine, theirs):
    top = jnp.maximum(mine[0], theirs[0])
    mine_by, theirs_by = jnp.exp2(mine[0] - top), jnp.exp2(theirs[0] - top)
    return jnp.stack([top, mine[1] * mine_by + theirs[1] * theirs_by, mine[2] * mine_by + theirs[2] * theirs_by])


def local(span_order, queries, key_rows, value_rows, out_grads):
    q_own, kv_own = call_pack(queries, key_rows, value_rows, out_grads)
    q_got = [back(q_own, "y", k) for k in (1, 2, 3)]
    kv1, kv3 = back(kv_own, "z", 1), back(kv_own, "z", 3)
    kv_again, kv1, kv3 = lax.optimization_barrier((kv_own, kv1, kv3))
    kv2 = back(kv_again, "z", 2)
    q_got, kv2 = lax.optimization_barrier((q_got, kv2))
    q_near = jnp.concatenate([q_own] + q_got, axis=0)
    q_far = swap_core(q_near)
    kvs = [kv_own, kv1, kv2, kv3]

    stats = call_stats(False, span_order, q_near, kvs)
    stats = call_stats(True, span_order, q_far, kvs, stats)
    stats = merged(stats, swap_core(stats))
    stats = [stats] + [back(stats, "y", k) for k in (1, 2, 3)]

    common = (span_order, stats, q_near, q_far, kvs)
    (dkv1, dkv2, dkv3), (dqt,) = call_grads((1, 2, 3), True, False, *common, None)
    (dkv0,), (dq_keep, dq_send) = call_grads((0,), False, True, *common, dqt)
    z1, z2, z3 = ahead(dkv1, "z", 1), ahead(dkv2, "z", 2), ahead(dkv3, "z", 3)
    (summed,) = plain_call(middle_kernel, "middle", [((PIECE, DH), BF16)], dkv0, z1, z2, z3)
    dq_send, summed = lax.optimization_barrier((dq_send, summed))
    dq_other = swap_core(dq_send)
    rows = (2 * SPAN, DH)
    dq, r1, r2, r3 = plain_call(
        query_kernel, "query", [(rows, F32), (rows, BF16), (rows, BF16), (rows, BF16)], dq_keep, dq_other
    )
    xs = [back(summed, "x", k) for k in (1, 2, 3)]
    ys = [ahead(part, "y", k) for k, part in ((1, r1), (2, r2), (3, r3))]
    return plain_call(last_kernel, "last", [(rows, BF16)] * 3, summed, *xs, dq, *ys)


def solution(mesh):
    fine = Mesh(mesh.devices.reshape(4, 4, 2, 4), ("z", "y", "c", "x"))
    ctx = ("z", "y", "c")
    return jax.shard_map(
        local,
        mesh=fine,
        in_specs=(P(), P(ctx, "x"), P(ctx, None), P(ctx, None), P(ctx, "x")),
        out_specs=(P(ctx, "x"), P(ctx, None), P(ctx, None)),
        check_vma=False,
    )
```

```python
import functools

import jax
import jax.numpy as jnp
from jax import lax
from jax.experimental import pallas as pl
from jax.experimental.pallas import tpu as pltpu
from jax.sharding import Mesh, PartitionSpec as P

DH = 128
SPAN = 256
SCALE = DH ** (-0.5)
LOG2E = 1.4426950408889634
SCALE2 = SCALE * LOG2E
NEG = -1e30
NT = (((1,), (1,)), ((), ()))
NN = (((1,), (0,)), ((), ()))
F32 = jnp.float32
BF16 = jnp.bfloat16


def spans_of(order_ref, z, y, c):
    row = (z * 4 + y) * 2 + c
    first, second = order_ref[row, 0], order_ref[row, 1]
    return jnp.minimum(first, second), jnp.where(first < second, 0, 1)


def query_spans(order_ref, a):
    z, y, c = lax.axis_index("z"), lax.axis_index("y"), lax.axis_index("c")
    return spans_of(order_ref, z, (y + 4 - a % 4) % 4, (c + a // 4) % 2)


def key_spans(order_ref, b):
    z, y, c = lax.axis_index("z"), lax.axis_index("y"), lax.axis_index("c")
    return spans_of(order_ref, (z + 4 - b) % 4, y, c)


def one_query_piece(order_ref, tile, a, pieces, own):
    low, low_slot = query_spans(order_ref, a)
    found = [key_spans(order_ref, b) for b in pieces]
    tile(a, 1 - low_slot, [(b, slot) for b, (_, slot) in zip(pieces, found)], False)
    for b, (key_low, key_slot) in zip(pieces, found):
        if own and b == 0:
            tile(0, 0, [(0, 0)], True)
            tile(0, 1, [(0, 1)], True)
        else:
            lows = low > key_low
            tile(a, jnp.where(lows, low_slot, 1 - low_slot), [(b, jnp.where(lows, key_slot, 1 - key_slot))], False)


def half(ref, piece, which, second):
    begin = which * SPAN + second * 2 * SPAN
    if not isinstance(begin, int):
        begin = pl.multiple_of(begin, SPAN)
    return ref[piece, pl.ds(begin, SPAN), :]


def products(q_ref, kv_ref, a, q_which, b, k_which):
    scores = lax.dot_general(
        half(kv_ref, b, k_which, 0), half(q_ref, a, q_which, 0), NT, preferred_element_type=F32
    )
    dprobs = lax.dot_general(
        half(kv_ref, b, k_which, 1), half(q_ref, a, q_which, 1), NT, preferred_element_type=F32
    )
    return scores * SCALE2, dprobs


def diagonal_visible():
    key_row = lax.broadcasted_iota(jnp.int32, (SPAN, SPAN), 0)
    query_row = lax.broadcasted_iota(jnp.int32, (SPAN, SPAN), 1)
    return key_row <= query_row


def query_place(a):
    y, c = lax.axis_index("y"), lax.axis_index("c")
    return 2 * (((y + 4 - a % 4) % 4) * 2 + (c + a // 4) % 2)


def in_flight(begin, finish, depth):
    waiting = []

    def tile(a, q_which, keys, masked):
        for b, k_which in keys:
            waiting.append(begin(a, q_which, b, k_which, masked))
            if len(waiting) > depth:
                finish(waiting.pop(0))

    def drain():
        while waiting:
            finish(waiting.pop(0))

    return tile, drain


def stats_kernel(far, order_ref, q_ref, *refs):
    kv_refs, refs = refs[:4], refs[4:]
    if far:
        before_ref, refs = refs[0], refs[1:]
    out_ref, kv_ref, top_ref, total_ref, weighted_ref = refs
    if far:
        out_ref[...] = before_ref[...]
    for b, ref in enumerate(kv_refs):
        kv_ref[b] = ref[...]
    top_ref[...] = jnp.full(top_ref.shape, NEG, F32)
    total_ref[...] = jnp.zeros(total_ref.shape, F32)
    weighted_ref[...] = jnp.zeros(weighted_ref.shape, F32)
    base = 4 if far else 0
    pieces = (0, 1, 2, 3)

    def begin(a, q_which, b, k_which, masked):
        scores, dprobs = products(q_ref, kv_ref, a - base, q_which, b, k_which)
        if masked:
            scores = jnp.where(diagonal_visible(), scores, NEG)
        return (a - base) * 2 + q_which, masked, scores.reshape(32, 8, SPAN), dprobs.reshape(32, 8, SPAN)

    def finish(state):
        slot, masked, scores, dprobs = state
        old = top_ref[slot]
        top = jnp.maximum(old, jnp.max(scores, axis=0))
        shrink = jnp.exp2(old - top)
        expon = jnp.exp2(scores - top[None])
        if masked:
            expon = jnp.where(diagonal_visible().reshape(32, 8, SPAN), expon, 0.0)
        top_ref[slot] = top
        total_ref[slot] = total_ref[slot] * shrink + jnp.sum(expon, axis=0)
        weighted_ref[slot] = weighted_ref[slot] * shrink + jnp.sum(expon * dprobs, axis=0)

    tile, drain = in_flight(begin, finish, 2)
    for a in range(base, base + 4):
        one_query_piece(order_ref, tile, a, pieces, a == 0)
    drain()
    for slot in range(8):
        tops = top_ref[slot]
        top = jnp.max(tops, axis=0, keepdims=True)
        factor = jnp.exp2(tops - top)
        rows = (
            top,
            jnp.sum(total_ref[slot] * factor, axis=0, keepdims=True),
            jnp.sum(weighted_ref[slot] * factor, axis=0, keepdims=True),
        )
        place = query_place(base + slot // 2) + slot % 2
        for kind, row in enumerate(rows):
            out_ref[kind, pl.ds(place, 1), :] = row


def norm_and_delta(stat_refs, sum_ref, norm_ref, delta_ref):
    found = [[ref[kind] for kind in range(3)] for ref in stat_refs]
    top = functools.reduce(jnp.maximum, [f[0] for f in found])
    factors = [jnp.exp2(f[0] - top) for f in found]
    total = sum(f[1] * g for f, g in zip(found, factors))
    sum_ref[0] = top + jnp.log2(total)
    sum_ref[1] = sum(f[2] * g for f, g in zip(found, factors)) / total
    for slot in range(16):
        place = query_place(slot // 2) + slot % 2
        norm_ref[slot] = jnp.broadcast_to(sum_ref[0, pl.ds(place, 1), :], (8, SPAN))
        delta_ref[slot] = jnp.broadcast_to(sum_ref[1, pl.ds(place, 1), :], (8, SPAN))


def grads_kernel(pieces, first, last, *refs):
    refs = list(refs)
    order_ref, stat_refs, near_ref, far_ref = refs[0], refs[1:5], refs[5], refs[6]
    del refs[:7]
    kv_refs = refs[: len(pieces)]
    del refs[: len(pieces)]
    dqt_in = None if first else refs.pop(0)
    dkv_refs = [refs.pop(0) for _ in dkv_parts(pieces)]
    dq_outs = [refs.pop(0), refs.pop(0)] if last else [refs.pop(0)]
    kv_ref, sum_ref, norm_ref, delta_ref, dk_ref, dv_ref, kt_ref = refs[:7]
    dqt_ref = refs[7] if last else dq_outs[0]

    norm_and_delta(stat_refs, sum_ref, norm_ref, delta_ref)
    for i, b in enumerate(pieces):
        kv_ref[i] = kv_refs[i][...]
        for which in range(2):
            kt_ref[2 * i + which] = kv_ref[i, pl.ds(which * SPAN, SPAN), :].T
    dk_ref[...] = jnp.zeros(dk_ref.shape, F32)
    dv_ref[...] = jnp.zeros(dv_ref.shape, F32)
    if first:
        dqt_ref[...] = jnp.zeros(dqt_ref.shape, F32)
    else:
        dqt_ref[...] = dqt_in[...]

    def begin(a, q_which, b, k_which, masked):
        slot = a * 2 + q_which
        q_ref, base = source
        queries = half(q_ref, a - base, q_which, 0)
        out_grads = half(q_ref, a - base, q_which, 1)
        i = pieces.index(b)
        scores = lax.dot_general(
            half(kv_ref, i, k_which, 0), queries, NT, preferred_element_type=F32
        ) * SCALE2
        dprobs = lax.dot_general(
            half(kv_ref, i, k_which, 1), out_grads, NT, preferred_element_type=F32
        )
        return slot, 2 * i + k_which, masked, queries, out_grads, scores, dprobs

    def finish(state):
        slot, key_slot, masked, queries, out_grads, scores, dprobs = state
        probs = jnp.exp2(scores.reshape(32, 8, SPAN) - norm_ref[slot][None])
        if masked:
            probs = jnp.where(diagonal_visible().reshape(32, 8, SPAN), probs, 0.0)
        dscores = probs * (dprobs.reshape(32, 8, SPAN) - delta_ref[slot][None])
        probs = probs.reshape(SPAN, SPAN).astype(BF16)
        dscores = dscores.reshape(SPAN, SPAN).astype(BF16)
        dv_ref[key_slot] += lax.dot_general(probs, out_grads, NN, preferred_element_type=F32)
        dk_ref[key_slot] += lax.dot_general(dscores, queries, NN, preferred_element_type=F32)
        dqt_ref[slot] += lax.dot_general(kt_ref[key_slot], dscores, NN, preferred_element_type=F32)

    tile, drain = in_flight(begin, finish, 1)
    for source in ((near_ref, 0), (far_ref, 4)):
        for a in range(source[1], source[1] + 4):
            one_query_piece(order_ref, tile, a, pieces, a == 0 and 0 in pieces)
    drain()
    parts = [ref for i in range(len(pieces)) for ref in (dk_ref.at[2 * i], dk_ref.at[2 * i + 1], dv_ref.at[2 * i], dv_ref.at[2 * i + 1])]
    for ref in dkv_refs:
        for j in range(ref.shape[0] // SPAN):
            ref[pl.ds(j * SPAN, SPAN), :] = parts.pop(0)[...].astype(ref.dtype)
    if last:
        for out, first_slot in zip(dq_outs, (0, 8)):
            out[...] = dqt_ref[first_slot : first_slot + 8].astype(out.dtype)


def pack_kernel(queries_ref, keys_ref, values_ref, grads_ref, q_ref, kv_ref, sems):
    rows = 2 * SPAN
    copies = []
    for i, (source, target) in enumerate(
        ((queries_ref, q_ref), (grads_ref, q_ref), (keys_ref, kv_ref), (values_ref, kv_ref))
    ):
        place = target.at[pl.ds((i % 2) * rows, rows), :]
        copies.append(pltpu.make_async_copy(source, place, sems.at[i]))
    for copy in copies:
        copy.start()
    for copy in copies:
        copy.wait()


def relay_kernel(dkv1_ref, dkv3_ref, keys_ref, values_ref, out1_ref, out3_ref):
    keys, values = pl.ds(0, 2 * SPAN), pl.ds(2 * SPAN, 2 * SPAN)
    out1_ref[keys, :] = (dkv1_ref[keys, :] + keys_ref[...].astype(F32)).astype(BF16)
    out1_ref[values, :] = dkv1_ref[values, :].astype(BF16)
    out3_ref[keys, :] = dkv3_ref[keys, :].astype(BF16)
    out3_ref[values, :] = (dkv3_ref[values, :] + values_ref[...].astype(F32)).astype(BF16)


def middle_kernel(dkv_ref, z1_ref, z3_ref, sum_ref):
    total = dkv_ref[...] + z1_ref[...].astype(F32) + z3_ref[...].astype(F32)
    sum_ref[...] = total.astype(BF16)


def query_kernel(keep_ref, other_ref, dq_ref, r1_ref, r2_ref, r3_ref):
    for k, ref in enumerate((dq_ref, r1_ref, r2_ref, r3_ref)):
        slots = pl.ds(2 * k, 2)
        ref[...] = (keep_ref[slots] + other_ref[slots].astype(F32)).astype(ref.dtype)


def last_kernel(sum_ref, x1_ref, x2_ref, x3_ref, dq_ref, y1_ref, y2_ref, y3_ref, q_out, k_out, v_out):
    own, x1, x2, x3 = [ref[...].astype(F32) for ref in (sum_ref, x1_ref, x2_ref, x3_ref)]
    total = (own + x2) + (x1 + x3)
    k_out[...] = (total[: 2 * SPAN] * SCALE).astype(BF16)
    v_out[...] = total[2 * SPAN :].astype(BF16)
    dq = dq_ref[...]
    for ref in (y1_ref, y2_ref, y3_ref):
        dq = dq + ref[...].astype(F32)
    for slot in range(2):
        q_out[pl.ds(slot * SPAN, SPAN), :] = (dq[slot] * SCALE).T.astype(BF16)


SMEM = pl.BlockSpec(memory_space=pltpu.SMEM)
VMEM = pl.BlockSpec(memory_space=pltpu.VMEM)
PIECE = 4 * SPAN


def call_stats(far, span_order, q_pieces, kvs, *before):
    args = [span_order, q_pieces.reshape(4, PIECE, DH), *kvs, *before]
    return pl.pallas_call(
        functools.partial(stats_kernel, far),
        out_shape=jax.ShapeDtypeStruct((3, 16, SPAN), F32),
        in_specs=[SMEM] + [VMEM] * (len(args) - 1),
        out_specs=VMEM,
        scratch_shapes=[pltpu.VMEM((4, PIECE, DH), BF16)] + [pltpu.VMEM((8, 8, SPAN), F32)] * 3,
        compiler_params=pltpu.CompilerParams(vmem_limit_bytes=32 * 2**20),
        cost_estimate=pl.CostEstimate(
            flops=32 * 2 * 2 * SPAN * SPAN * DH, bytes_accessed=2**21, transcendentals=32 * SPAN * SPAN
        ),
        name="stats",
    )(*args)


def dkv_parts(pieces):
    if pieces == (2,):
        return (jax.ShapeDtypeStruct((PIECE // 2, DH), BF16),) * 2
    return (jax.ShapeDtypeStruct((PIECE, DH), F32),) * len(pieces)


def call_grads(pieces, first, last, span_order, stats, q_near, q_far, kvs, dqt):
    tiles = 16 * len(pieces)
    dkv_shapes = dkv_parts(pieces)
    if last:
        dq_shapes = tuple(jax.ShapeDtypeStruct((8, DH, SPAN), dtype) for dtype in (F32, BF16))
    else:
        dq_shapes = (jax.ShapeDtypeStruct((16, DH, SPAN), F32),)
    q_pieces = [q.reshape(4, PIECE, DH) for q in (q_near, q_far)]
    args = [span_order, *stats, *q_pieces, *[kvs[b] for b in pieces]] + ([] if first else [dqt])
    out = pl.pallas_call(
        functools.partial(grads_kernel, pieces, first, last),
        out_shape=dkv_shapes + dq_shapes,
        in_specs=[SMEM] + [VMEM] * (len(args) - 1),
        out_specs=(VMEM,) * (len(dkv_shapes) + len(dq_shapes)),
        scratch_shapes=[
            pltpu.VMEM((len(pieces), PIECE, DH), BF16),
            pltpu.VMEM((2, 16, SPAN), F32),
            pltpu.VMEM((16, 8, SPAN), F32),
            pltpu.VMEM((16, 8, SPAN), F32),
            pltpu.VMEM((2 * len(pieces), SPAN, DH), F32),
            pltpu.VMEM((2 * len(pieces), SPAN, DH), F32),
            pltpu.VMEM((2 * len(pieces), DH, SPAN), BF16),
        ]
        + ([pltpu.VMEM((16, DH, SPAN), F32)] if last else []),
        compiler_params=pltpu.CompilerParams(vmem_limit_bytes=32 * 2**20),
        cost_estimate=pl.CostEstimate(
            flops=tiles * 5 * 2 * SPAN * SPAN * DH, bytes_accessed=4 * 2**20, transcendentals=tiles * SPAN * SPAN
        ),
        name="grads",
    )(*args)
    return out[: len(dkv_shapes)], out[len(dkv_shapes) :]


def plain_call(kernel, name, out_shapes, *args):
    return pl.pallas_call(
        kernel,
        out_shape=tuple(jax.ShapeDtypeStruct(shape, dtype) for shape, dtype in out_shapes),
        in_specs=[VMEM] * len(args),
        out_specs=(VMEM,) * len(out_shapes),
        compiler_params=pltpu.CompilerParams(vmem_limit_bytes=16 * 2**20),
        cost_estimate=pl.CostEstimate(flops=2**20, bytes_accessed=2**21, transcendentals=0),
        name=name,
    )(*args)


def call_pack(*args):
    return pl.pallas_call(
        pack_kernel,
        out_shape=(jax.ShapeDtypeStruct((PIECE, DH), BF16),) * 2,
        in_specs=[pl.BlockSpec(memory_space=pl.ANY)] * 4,
        out_specs=(VMEM, VMEM),
        scratch_shapes=[pltpu.SemaphoreType.DMA((4,))],
        compiler_params=pltpu.CompilerParams(vmem_limit_bytes=56 * 2**20),
        name="pack",
    )(*args)


def back(value, axis, k):
    return lax.ppermute(value, axis, [(i, (i + k) % 4) for i in range(4)])


def ahead(value, axis, k):
    return lax.ppermute(value, axis, [(i, (i - k) % 4) for i in range(4)])


def swap_core(value):
    return lax.ppermute(value, "c", [(0, 1), (1, 0)])


def merged(mine, theirs):
    top = jnp.maximum(mine[0], theirs[0])
    mine_by, theirs_by = jnp.exp2(mine[0] - top), jnp.exp2(theirs[0] - top)
    return jnp.stack([top, mine[1] * mine_by + theirs[1] * theirs_by, mine[2] * mine_by + theirs[2] * theirs_by])


def local(span_order, queries, key_rows, value_rows, out_grads):
    q_own, kv_own = call_pack(queries, key_rows, value_rows, out_grads)
    q_got = [back(q_own, "y", k) for k in (1, 2, 3)]
    kv1, kv3 = back(kv_own, "z", 1), back(kv_own, "z", 3)
    kv_again, kv1, kv3 = lax.optimization_barrier((kv_own, kv1, kv3))
    kv2 = back(kv_again, "z", 2)
    q_got, kv2 = lax.optimization_barrier((q_got, kv2))
    q_near = jnp.concatenate([q_own] + q_got, axis=0)
    q_far = swap_core(q_near)
    kvs = [kv_own, kv1, kv2, kv3]

    stats = call_stats(False, span_order, q_near, kvs)
    stats = call_stats(True, span_order, q_far, kvs, stats)
    stats = merged(stats, swap_core(stats))
    stats = [stats] + [back(stats, "y", k) for k in (1, 2, 3)]

    common = (span_order, stats, q_near, q_far, kvs)
    (dk2, dv2), (dqt,) = call_grads((2,), True, False, *common, None)
    dk_relay, dv_relay = ahead(dk2, "z", 1), ahead(dv2, "z", 3)
    (dkv1, dkv3), (dqt,) = call_grads((1, 3), False, False, *common, dqt)
    dkv1, dkv3 = plain_call(relay_kernel, "relay", [((PIECE, DH), BF16)] * 2, dkv1, dkv3, dk_relay, dv_relay)
    (dkv0,), (dq_keep, dq_send) = call_grads((0,), False, True, *common, dqt)
    z1, z3 = ahead(dkv1, "z", 1), ahead(dkv3, "z", 3)
    (summed,) = plain_call(middle_kernel, "middle", [((PIECE, DH), BF16)], dkv0, z1, z3)
    dq_send, summed = lax.optimization_barrier((dq_send, summed))
    dq_other = swap_core(dq_send)
    rows, slots = (2 * SPAN, DH), (2, DH, SPAN)
    dq, r1, r2, r3 = plain_call(
        query_kernel, "query", [(slots, F32), (slots, BF16), (slots, BF16), (slots, BF16)], dq_keep, dq_other
    )
    xs = [back(summed, "x", k) for k in (1, 2, 3)]
    ys = [ahead(part, "y", k) for k, part in ((1, r1), (2, r2), (3, r3))]
    return plain_call(last_kernel, "last", [(rows, BF16)] * 3, summed, *xs, dq, *ys)


def solution(mesh):
    fine = Mesh(mesh.devices.reshape(4, 4, 2, 4), ("z", "y", "c", "x"))
    ctx = ("z", "y", "c")
    return jax.shard_map(
        local,
        mesh=fine,
        in_specs=(P(), P(ctx, "x"), P(ctx, None), P(ctx, None), P(ctx, "x")),
        out_specs=(P(ctx, "x"), P(ctx, None), P(ctx, None)),
        check_vma=False,
    )
```

```python
import functools

import jax
import jax.numpy as jnp
from jax import lax
from jax.experimental import pallas as pl
from jax.experimental.pallas import tpu as pltpu
from jax.sharding import Mesh, PartitionSpec as P

DH = 128
SPAN = 256
SCALE = DH ** (-0.5)
LOG2E = 1.4426950408889634
SCALE2 = SCALE * LOG2E
NEG = -1e30
NT = (((1,), (1,)), ((), ()))
NN = (((1,), (0,)), ((), ()))
F32 = jnp.float32
BF16 = jnp.bfloat16


def spans_of(order_ref, z, y, c):
    row = (z * 4 + y) * 2 + c
    first, second = order_ref[row, 0], order_ref[row, 1]
    return jnp.minimum(first, second), jnp.where(first < second, 0, 1)


def query_spans(order_ref, a):
    z, y, c = lax.axis_index("z"), lax.axis_index("y"), lax.axis_index("c")
    return spans_of(order_ref, z, (y + 4 - a % 4) % 4, (c + a // 4) % 2)


def key_spans(order_ref, b):
    z, y, c = lax.axis_index("z"), lax.axis_index("y"), lax.axis_index("c")
    return spans_of(order_ref, (z + 4 - b) % 4, y, c)


def one_query_piece(order_ref, tile, a, pieces, own):
    low, low_slot = query_spans(order_ref, a)
    found = [key_spans(order_ref, b) for b in pieces]
    tile(a, 1 - low_slot, [(b, slot) for b, (_, slot) in zip(pieces, found)], False)
    for b, (key_low, key_slot) in zip(pieces, found):
        if own and b == 0:
            tile(0, 0, [(0, 0)], True)
            tile(0, 1, [(0, 1)], True)
        else:
            lows = low > key_low
            tile(a, jnp.where(lows, low_slot, 1 - low_slot), [(b, jnp.where(lows, key_slot, 1 - key_slot))], False)


def half(ref, piece, which, second):
    begin = which * SPAN + second * 2 * SPAN
    if not isinstance(begin, int):
        begin = pl.multiple_of(begin, SPAN)
    return ref[piece, pl.ds(begin, SPAN), :]


def products(q_ref, kv_ref, a, q_which, b, k_which):
    scores = lax.dot_general(
        half(kv_ref, b, k_which, 0), half(q_ref, a, q_which, 0), NT, preferred_element_type=F32
    )
    dprobs = lax.dot_general(
        half(kv_ref, b, k_which, 1), half(q_ref, a, q_which, 1), NT, preferred_element_type=F32
    )
    return scores * SCALE2, dprobs


def diagonal_visible():
    key_row = lax.broadcasted_iota(jnp.int32, (SPAN, SPAN), 0)
    query_row = lax.broadcasted_iota(jnp.int32, (SPAN, SPAN), 1)
    return key_row <= query_row


def query_place(a):
    y, c = lax.axis_index("y"), lax.axis_index("c")
    return 2 * (((y + 4 - a % 4) % 4) * 2 + (c + a // 4) % 2)


def in_flight(begin, finish, depth):
    waiting = []

    def tile(a, q_which, keys, masked):
        for b, k_which in keys:
            waiting.append(begin(a, q_which, b, k_which, masked))
            if len(waiting) > depth:
                finish(waiting.pop(0))

    def drain():
        while waiting:
            finish(waiting.pop(0))

    return tile, drain


def stats_kernel(far, order_ref, q_ref, *refs):
    kv_refs, refs = refs[:4], refs[4:]
    if far:
        before_ref, refs = refs[0], refs[1:]
    out_ref, kv_ref, top_ref, total_ref, weighted_ref = refs
    if far:
        out_ref[...] = before_ref[...]
    for b, ref in enumerate(kv_refs):
        kv_ref[b] = ref[...]
    top_ref[...] = jnp.full(top_ref.shape, NEG, F32)
    total_ref[...] = jnp.zeros(total_ref.shape, F32)
    weighted_ref[...] = jnp.zeros(weighted_ref.shape, F32)
    base = 4 if far else 0
    pieces = (0, 1, 2, 3)

    def begin(a, q_which, b, k_which, masked):
        scores, dprobs = products(q_ref, kv_ref, a - base, q_which, b, k_which)
        if masked:
            scores = jnp.where(diagonal_visible(), scores, NEG)
        return (a - base) * 2 + q_which, masked, scores.reshape(32, 8, SPAN), dprobs.reshape(32, 8, SPAN)

    def finish(state):
        slot, masked, scores, dprobs = state
        old = top_ref[slot]
        top = jnp.maximum(old, jnp.max(scores, axis=0))
        shrink = jnp.exp2(old - top)
        expon = jnp.exp2(scores - top[None])
        if masked:
            expon = jnp.where(diagonal_visible().reshape(32, 8, SPAN), expon, 0.0)
        top_ref[slot] = top
        total_ref[slot] = total_ref[slot] * shrink + jnp.sum(expon, axis=0)
        weighted_ref[slot] = weighted_ref[slot] * shrink + jnp.sum(expon * dprobs, axis=0)

    tile, drain = in_flight(begin, finish, 2)
    for a in range(base, base + 4):
        one_query_piece(order_ref, tile, a, pieces, a == 0)
    drain()
    for slot in range(8):
        tops = top_ref[slot]
        top = jnp.max(tops, axis=0, keepdims=True)
        factor = jnp.exp2(tops - top)
        rows = (
            top,
            jnp.sum(total_ref[slot] * factor, axis=0, keepdims=True),
            jnp.sum(weighted_ref[slot] * factor, axis=0, keepdims=True),
        )
        place = query_place(base + slot // 2) + slot % 2
        for kind, row in enumerate(rows):
            out_ref[kind, pl.ds(place, 1), :] = row


def norm_and_delta(stat_refs, sum_ref, norm_ref, delta_ref):
    found = [[ref[kind] for kind in range(3)] for ref in stat_refs]
    top = functools.reduce(jnp.maximum, [f[0] for f in found])
    factors = [jnp.exp2(f[0] - top) for f in found]
    total = sum(f[1] * g for f, g in zip(found, factors))
    sum_ref[0] = top + jnp.log2(total)
    sum_ref[1] = sum(f[2] * g for f, g in zip(found, factors)) / total
    for slot in range(16):
        place = query_place(slot // 2) + slot % 2
        norm_ref[slot] = jnp.broadcast_to(sum_ref[0, pl.ds(place, 1), :], (8, SPAN))
        delta_ref[slot] = jnp.broadcast_to(sum_ref[1, pl.ds(place, 1), :], (8, SPAN))


def grads_kernel(pieces, first, last, *refs):
    refs = list(refs)
    order_ref, stat_refs, near_ref, far_ref = refs[0], refs[1:5], refs[5], refs[6]
    del refs[:7]
    kv_refs = refs[: len(pieces)]
    del refs[: len(pieces)]
    dqt_in = None if first else refs.pop(0)
    dkv_refs = [refs.pop(0) for _ in dkv_parts(pieces)]
    dq_outs = [refs.pop(0), refs.pop(0)] if last else [refs.pop(0)]
    kv_ref, sum_ref, norm_ref, delta_ref, dk_ref, dv_ref, kt_ref = refs[:7]
    dqt_ref = refs[7] if last else dq_outs[0]

    norm_and_delta(stat_refs, sum_ref, norm_ref, delta_ref)
    for i, b in enumerate(pieces):
        kv_ref[i] = kv_refs[i][...]
        for which in range(2):
            kt_ref[2 * i + which] = kv_ref[i, pl.ds(which * SPAN, SPAN), :].T
    dk_ref[...] = jnp.zeros(dk_ref.shape, F32)
    dv_ref[...] = jnp.zeros(dv_ref.shape, F32)
    if first:
        dqt_ref[...] = jnp.zeros(dqt_ref.shape, F32)
    else:
        dqt_ref[...] = dqt_in[...]

    def begin(a, q_which, b, k_which, masked):
        slot = a * 2 + q_which
        q_ref, base = source
        queries = half(q_ref, a - base, q_which, 0)
        out_grads = half(q_ref, a - base, q_which, 1)
        i = pieces.index(b)
        scores = lax.dot_general(
            half(kv_ref, i, k_which, 0), queries, NT, preferred_element_type=F32
        ) * SCALE2
        dprobs = lax.dot_general(
            half(kv_ref, i, k_which, 1), out_grads, NT, preferred_element_type=F32
        )
        return slot, 2 * i + k_which, masked, queries, out_grads, scores, dprobs

    def finish(state):
        slot, key_slot, masked, queries, out_grads, scores, dprobs = state
        probs = jnp.exp2(scores.reshape(32, 8, SPAN) - norm_ref[slot][None])
        if masked:
            probs = jnp.where(diagonal_visible().reshape(32, 8, SPAN), probs, 0.0)
        dscores = probs * (dprobs.reshape(32, 8, SPAN) - delta_ref[slot][None])
        probs = probs.reshape(SPAN, SPAN).astype(BF16)
        dscores = dscores.reshape(SPAN, SPAN).astype(BF16)
        dv_ref[key_slot] += lax.dot_general(probs, out_grads, NN, preferred_element_type=F32)
        dk_ref[key_slot] += lax.dot_general(dscores, queries, NN, preferred_element_type=F32)
        dqt_ref[slot] += lax.dot_general(kt_ref[key_slot], dscores, NN, preferred_element_type=F32)

    tile, drain = in_flight(begin, finish, 1)
    for source in ((near_ref, 0), (far_ref, 4)):
        for a in range(source[1], source[1] + 4):
            one_query_piece(order_ref, tile, a, pieces, a == 0 and 0 in pieces)
    drain()
    parts = [ref for i in range(len(pieces)) for ref in (dk_ref.at[2 * i], dk_ref.at[2 * i + 1], dv_ref.at[2 * i], dv_ref.at[2 * i + 1])]
    for ref in dkv_refs:
        for j in range(ref.shape[0] // SPAN):
            ref[pl.ds(j * SPAN, SPAN), :] = parts.pop(0)[...].astype(ref.dtype)
    if last:
        for out, first_slot in zip(dq_outs, (0, 8)):
            out[...] = dqt_ref[first_slot : first_slot + 8].astype(out.dtype)


def pack_kernel(queries_ref, keys_ref, values_ref, grads_ref, q_ref, kv_ref, sems):
    rows = 2 * SPAN
    copies = []
    for i, (source, target) in enumerate(
        ((queries_ref, q_ref), (grads_ref, q_ref), (keys_ref, kv_ref), (values_ref, kv_ref))
    ):
        place = target.at[pl.ds((i % 2) * rows, rows), :]
        copies.append(pltpu.make_async_copy(source, place, sems.at[i]))
    for copy in copies:
        copy.start()
    for copy in copies:
        copy.wait()


def relay_kernel(dkv1_ref, dkv3_ref, keys_ref, values_ref, out1_ref, out3_ref):
    keys, values = pl.ds(0, 2 * SPAN), pl.ds(2 * SPAN, 2 * SPAN)
    out1_ref[keys, :] = (dkv1_ref[keys, :] + keys_ref[...].astype(F32)).astype(BF16)
    out1_ref[values, :] = dkv1_ref[values, :].astype(BF16)
    out3_ref[keys, :] = dkv3_ref[keys, :].astype(BF16)
    out3_ref[values, :] = (dkv3_ref[values, :] + values_ref[...].astype(F32)).astype(BF16)


def middle_kernel(dkv_ref, z1_ref, z3_ref, sum_ref):
    total = dkv_ref[...] + z1_ref[...].astype(F32) + z3_ref[...].astype(F32)
    sum_ref[...] = total.astype(BF16)


def query_kernel(keep_ref, other_ref, dq_ref, r1_ref, r3_ref, first_ref, second_ref):
    for k, ref in ((0, dq_ref), (1, r1_ref), (3, r3_ref)):
        slots = pl.ds(2 * k, 2)
        ref[...] = keep_ref[slots] + other_ref[slots].astype(F32)
    for slot, ref in ((4, first_ref), (5, second_ref)):
        ref[...] = (keep_ref[slot] + other_ref[slot].astype(F32)).astype(BF16)


def query_relay_kernel(r1_ref, r3_ref, first_ref, second_ref, out1_ref, out3_ref):
    out1_ref[0] = (r1_ref[0] + first_ref[...].astype(F32)).astype(BF16)
    out1_ref[1] = r1_ref[1].astype(BF16)
    out3_ref[0] = r3_ref[0].astype(BF16)
    out3_ref[1] = (r3_ref[1] + second_ref[...].astype(F32)).astype(BF16)


def last_kernel(sum_ref, x1_ref, x2_ref, x3_ref, dq_ref, y1_ref, y3_ref, q_out, k_out, v_out):
    own, x1, x2, x3 = [ref[...].astype(F32) for ref in (sum_ref, x1_ref, x2_ref, x3_ref)]
    total = (own + x2) + (x1 + x3)
    k_out[...] = (total[: 2 * SPAN] * SCALE).astype(BF16)
    v_out[...] = total[2 * SPAN :].astype(BF16)
    dq = dq_ref[...]
    for ref in (y1_ref, y3_ref):
        dq = dq + ref[...].astype(F32)
    for slot in range(2):
        q_out[pl.ds(slot * SPAN, SPAN), :] = (dq[slot] * SCALE).T.astype(BF16)


SMEM = pl.BlockSpec(memory_space=pltpu.SMEM)
VMEM = pl.BlockSpec(memory_space=pltpu.VMEM)
PIECE = 4 * SPAN


def call_stats(far, span_order, q_pieces, kvs, *before):
    args = [span_order, q_pieces.reshape(4, PIECE, DH), *kvs, *before]
    return pl.pallas_call(
        functools.partial(stats_kernel, far),
        out_shape=jax.ShapeDtypeStruct((3, 16, SPAN), F32),
        in_specs=[SMEM] + [VMEM] * (len(args) - 1),
        out_specs=VMEM,
        scratch_shapes=[pltpu.VMEM((4, PIECE, DH), BF16)] + [pltpu.VMEM((8, 8, SPAN), F32)] * 3,
        compiler_params=pltpu.CompilerParams(vmem_limit_bytes=32 * 2**20),
        cost_estimate=pl.CostEstimate(
            flops=32 * 2 * 2 * SPAN * SPAN * DH, bytes_accessed=2**21, transcendentals=32 * SPAN * SPAN
        ),
        name="stats",
    )(*args)


def dkv_parts(pieces):
    if pieces == (2,):
        return (jax.ShapeDtypeStruct((PIECE // 2, DH), BF16),) * 2
    return (jax.ShapeDtypeStruct((PIECE, DH), F32),) * len(pieces)


def call_grads(pieces, first, last, span_order, stats, q_near, q_far, kvs, dqt):
    tiles = 16 * len(pieces)
    dkv_shapes = dkv_parts(pieces)
    if last:
        dq_shapes = tuple(jax.ShapeDtypeStruct((8, DH, SPAN), dtype) for dtype in (F32, BF16))
    else:
        dq_shapes = (jax.ShapeDtypeStruct((16, DH, SPAN), F32),)
    q_pieces = [q.reshape(4, PIECE, DH) for q in (q_near, q_far)]
    args = [span_order, *stats, *q_pieces, *[kvs[b] for b in pieces]] + ([] if first else [dqt])
    out = pl.pallas_call(
        functools.partial(grads_kernel, pieces, first, last),
        out_shape=dkv_shapes + dq_shapes,
        in_specs=[SMEM] + [VMEM] * (len(args) - 1),
        out_specs=(VMEM,) * (len(dkv_shapes) + len(dq_shapes)),
        scratch_shapes=[
            pltpu.VMEM((len(pieces), PIECE, DH), BF16),
            pltpu.VMEM((2, 16, SPAN), F32),
            pltpu.VMEM((16, 8, SPAN), F32),
            pltpu.VMEM((16, 8, SPAN), F32),
            pltpu.VMEM((2 * len(pieces), SPAN, DH), F32),
            pltpu.VMEM((2 * len(pieces), SPAN, DH), F32),
            pltpu.VMEM((2 * len(pieces), DH, SPAN), BF16),
        ]
        + ([pltpu.VMEM((16, DH, SPAN), F32)] if last else []),
        compiler_params=pltpu.CompilerParams(vmem_limit_bytes=32 * 2**20),
        cost_estimate=pl.CostEstimate(
            flops=tiles * 5 * 2 * SPAN * SPAN * DH, bytes_accessed=4 * 2**20, transcendentals=tiles * SPAN * SPAN
        ),
        name="grads",
    )(*args)
    return out[: len(dkv_shapes)], out[len(dkv_shapes) :]


def plain_call(kernel, name, out_shapes, *args):
    return pl.pallas_call(
        kernel,
        out_shape=tuple(jax.ShapeDtypeStruct(shape, dtype) for shape, dtype in out_shapes),
        in_specs=[VMEM] * len(args),
        out_specs=(VMEM,) * len(out_shapes),
        compiler_params=pltpu.CompilerParams(vmem_limit_bytes=16 * 2**20),
        cost_estimate=pl.CostEstimate(flops=2**20, bytes_accessed=2**21, transcendentals=0),
        name=name,
    )(*args)


def call_pack(*args):
    return pl.pallas_call(
        pack_kernel,
        out_shape=(jax.ShapeDtypeStruct((PIECE, DH), BF16),) * 2,
        in_specs=[pl.BlockSpec(memory_space=pl.ANY)] * 4,
        out_specs=(VMEM, VMEM),
        scratch_shapes=[pltpu.SemaphoreType.DMA((4,))],
        compiler_params=pltpu.CompilerParams(vmem_limit_bytes=56 * 2**20),
        name="pack",
    )(*args)


def back(value, axis, k):
    return lax.ppermute(value, axis, [(i, (i + k) % 4) for i in range(4)])


def ahead(value, axis, k):
    return lax.ppermute(value, axis, [(i, (i - k) % 4) for i in range(4)])


def swap_core(value):
    return lax.ppermute(value, "c", [(0, 1), (1, 0)])


def merged(mine, theirs):
    top = jnp.maximum(mine[0], theirs[0])
    mine_by, theirs_by = jnp.exp2(mine[0] - top), jnp.exp2(theirs[0] - top)
    return jnp.stack([top, mine[1] * mine_by + theirs[1] * theirs_by, mine[2] * mine_by + theirs[2] * theirs_by])


def local(span_order, queries, key_rows, value_rows, out_grads):
    q_own, kv_own = call_pack(queries, key_rows, value_rows, out_grads)
    q_got = [back(q_own, "y", k) for k in (1, 2, 3)]
    kv1, kv3 = back(kv_own, "z", 1), back(kv_own, "z", 3)
    kv_again, kv1, kv3 = lax.optimization_barrier((kv_own, kv1, kv3))
    kv2 = back(kv_again, "z", 2)
    q_got, kv2 = lax.optimization_barrier((q_got, kv2))
    q_near = jnp.concatenate([q_own] + q_got, axis=0)
    q_far = swap_core(q_near)
    kvs = [kv_own, kv1, kv2, kv3]

    stats = call_stats(False, span_order, q_near, kvs)
    stats = call_stats(True, span_order, q_far, kvs, stats)
    stats = merged(stats, swap_core(stats))
    stats = [stats] + [back(stats, "y", k) for k in (1, 2, 3)]

    common = (span_order, stats, q_near, q_far, kvs)
    (dk2, dv2), (dqt,) = call_grads((2,), True, False, *common, None)
    dk_relay, dv_relay = ahead(dk2, "z", 1), ahead(dv2, "z", 3)
    (dkv1, dkv3), (dqt,) = call_grads((1, 3), False, False, *common, dqt)
    dkv1, dkv3 = plain_call(relay_kernel, "relay", [((PIECE, DH), BF16)] * 2, dkv1, dkv3, dk_relay, dv_relay)
    (dkv0,), (dq_keep, dq_send) = call_grads((0,), False, True, *common, dqt)
    z1, z3 = ahead(dkv1, "z", 1), ahead(dkv3, "z", 3)
    (summed,) = plain_call(middle_kernel, "middle", [((PIECE, DH), BF16)], dkv0, z1, z3)
    dq_send, summed = lax.optimization_barrier((dq_send, summed))
    dq_other = swap_core(dq_send)
    rows, slots = (2 * SPAN, DH), (2, DH, SPAN)
    one = (DH, SPAN)
    dq, r1, r3, first, second = plain_call(
        query_kernel, "query", [(slots, F32)] * 3 + [(one, BF16)] * 2, dq_keep, dq_other
    )
    r1, r3 = plain_call(
        query_relay_kernel, "query_relay", [(slots, BF16)] * 2, r1, r3, ahead(first, "y", 1), ahead(second, "y", 3)
    )
    xs = [back(summed, "x", k) for k in (1, 2, 3)]
    ys = [ahead(r1, "y", 1), ahead(r3, "y", 3)]
    return plain_call(last_kernel, "last", [(rows, BF16)] * 3, summed, *xs, dq, *ys)


def solution(mesh):
    fine = Mesh(mesh.devices.reshape(4, 4, 2, 4), ("z", "y", "c", "x"))
    ctx = ("z", "y", "c")
    return jax.shard_map(
        local,
        mesh=fine,
        in_specs=(P(), P(ctx, "x"), P(ctx, None), P(ctx, None), P(ctx, "x")),
        out_specs=(P(ctx, "x"), P(ctx, None), P(ctx, None)),
        check_vma=False,
    )
```

```python
import functools

import jax
import jax.numpy as jnp
from jax import lax
from jax.experimental import pallas as pl
from jax.experimental.pallas import tpu as pltpu
from jax.sharding import Mesh, PartitionSpec as P

DH = 128
SPAN = 256
SCALE = DH ** (-0.5)
LOG2E = 1.4426950408889634
SCALE2 = SCALE * LOG2E
NEG = -1e30
TINY = 1e-30
NT = (((1,), (1,)), ((), ()))
NN = (((1,), (0,)), ((), ()))
F32 = jnp.float32
BF16 = jnp.bfloat16


def spans_of(order_ref, z, y, c):
    row = (z * 4 + y) * 2 + c
    first, second = order_ref[row, 0], order_ref[row, 1]
    return jnp.minimum(first, second), jnp.where(first < second, 0, 1)


def query_spans(order_ref, a):
    z, y, c = lax.axis_index("z"), lax.axis_index("y"), lax.axis_index("c")
    return spans_of(order_ref, z, (y + 4 - a % 4) % 4, (c + a // 4) % 2)


def key_spans(order_ref, b):
    z, y, c = lax.axis_index("z"), lax.axis_index("y"), lax.axis_index("c")
    return spans_of(order_ref, (z + 4 - b) % 4, y, c)


def one_query_piece(order_ref, tile, a, pieces, own):
    low, low_slot = query_spans(order_ref, a)
    found = [key_spans(order_ref, b) for b in pieces]
    tile(a, 1 - low_slot, [(b, slot) for b, (_, slot) in zip(pieces, found)], False)
    for b, (key_low, key_slot) in zip(pieces, found):
        if own and b == 0:
            tile(0, 0, [(0, 0)], True)
            tile(0, 1, [(0, 1)], True)
        else:
            lows = low > key_low
            tile(a, jnp.where(lows, low_slot, 1 - low_slot), [(b, jnp.where(lows, key_slot, 1 - key_slot))], False)


def half(ref, piece, which, second):
    begin = which * SPAN + second * 2 * SPAN
    if not isinstance(begin, int):
        begin = pl.multiple_of(begin, SPAN)
    return ref[piece, pl.ds(begin, SPAN), :]


def products(q_ref, kv_ref, a, q_which, b, k_which):
    scores = lax.dot_general(
        half(kv_ref, b, k_which, 0), half(q_ref, a, q_which, 0), NT, preferred_element_type=F32
    )
    dprobs = lax.dot_general(
        half(kv_ref, b, k_which, 1), half(q_ref, a, q_which, 1), NT, preferred_element_type=F32
    )
    return scores * SCALE2, dprobs


def diagonal_visible():
    key_row = lax.broadcasted_iota(jnp.int32, (SPAN, SPAN), 0)
    query_row = lax.broadcasted_iota(jnp.int32, (SPAN, SPAN), 1)
    return key_row <= query_row


def query_place(a):
    y, c = lax.axis_index("y"), lax.axis_index("c")
    return 2 * (((y + 4 - a % 4) % 4) * 2 + (c + a // 4) % 2)


def in_flight(begin, finish, depth):
    waiting = []

    def tile(a, q_which, keys, masked):
        for b, k_which in keys:
            waiting.append(begin(a, q_which, b, k_which, masked))
            if len(waiting) > depth:
                finish(waiting.pop(0))

    def drain():
        while waiting:
            finish(waiting.pop(0))

    return tile, drain


def stats_kernel(far, order_ref, q_ref, *refs):
    kv_refs, refs = refs[:4], refs[4:]
    if far:
        before_ref, refs = refs[0], refs[1:]
    out_ref, kv_ref, top_ref, total_ref, weighted_ref = refs
    if far:
        out_ref[...] = before_ref[...]
    for b, ref in enumerate(kv_refs):
        kv_ref[b] = ref[...]
    top_ref[...] = jnp.full(top_ref.shape, NEG, F32)
    total_ref[...] = jnp.zeros(total_ref.shape, F32)
    weighted_ref[...] = jnp.zeros(weighted_ref.shape, F32)
    base = 4 if far else 0
    pieces = (0, 1, 2, 3)

    def begin(a, q_which, b, k_which, masked):
        scores, dprobs = products(q_ref, kv_ref, a - base, q_which, b, k_which)
        if masked:
            scores = jnp.where(diagonal_visible(), scores, NEG)
        return (a - base) * 2 + q_which, masked, scores.reshape(32, 8, SPAN), dprobs.reshape(32, 8, SPAN)

    def finish(state):
        slot, masked, scores, dprobs = state
        old = top_ref[slot]
        top = jnp.maximum(old, jnp.max(scores, axis=0))
        shrink = jnp.exp2(old - top)
        expon = jnp.exp2(scores - top[None])
        if masked:
            expon = jnp.where(diagonal_visible().reshape(32, 8, SPAN), expon, 0.0)
        top_ref[slot] = top
        total_ref[slot] = total_ref[slot] * shrink + jnp.sum(expon, axis=0)
        weighted_ref[slot] = weighted_ref[slot] * shrink + jnp.sum(expon * dprobs, axis=0)

    tile, drain = in_flight(begin, finish, 2)
    for a in range(base, base + 4):
        one_query_piece(order_ref, tile, a, pieces, a == 0)
    drain()
    for slot in range(8):
        tops = top_ref[slot]
        top = jnp.max(tops, axis=0, keepdims=True)
        factor = jnp.exp2(tops - top)
        rows = (
            top,
            jnp.sum(total_ref[slot] * factor, axis=0, keepdims=True),
            jnp.sum(weighted_ref[slot] * factor, axis=0, keepdims=True),
        )
        place = query_place(base + slot // 2) + slot % 2
        for kind, row in enumerate(rows):
            out_ref[kind, pl.ds(place, 1), :] = row


def norm_and_delta(stat_refs, sum_ref, norm_ref, delta_ref):
    found = [(ref[0], ref[1]) for ref in stat_refs]
    top = functools.reduce(jnp.maximum, [norm for norm, _ in found])
    factors = [jnp.exp2(norm - top) for norm, _ in found]
    total = sum(factors)
    sum_ref[0] = top + jnp.log2(total)
    sum_ref[1] = sum(delta * g for (_, delta), g in zip(found, factors)) / total
    for slot in range(16):
        place = query_place(slot // 2) + slot % 2
        norm_ref[slot] = jnp.broadcast_to(sum_ref[0, pl.ds(place, 1), :], (8, SPAN))
        delta_ref[slot] = jnp.broadcast_to(sum_ref[1, pl.ds(place, 1), :], (8, SPAN))


def grads_kernel(pieces, first, last, *refs):
    refs = list(refs)
    order_ref, stat_refs, near_ref, far_ref = refs[0], refs[1:5], refs[5], refs[6]
    del refs[:7]
    kv_refs = refs[: len(pieces)]
    del refs[: len(pieces)]
    dqt_in = None if first else refs.pop(0)
    dkv_refs = [refs.pop(0) for _ in dkv_parts(pieces)]
    dq_outs = [refs.pop(0), refs.pop(0)] if last else [refs.pop(0)]
    kv_ref, sum_ref, norm_ref, delta_ref, dk_ref, dv_ref, kt_ref = refs[:7]
    dqt_ref = refs[7] if last else dq_outs[0]

    norm_and_delta(stat_refs, sum_ref, norm_ref, delta_ref)
    for i, b in enumerate(pieces):
        kv_ref[i] = kv_refs[i][...]
        for which in range(2):
            kt_ref[2 * i + which] = kv_ref[i, pl.ds(which * SPAN, SPAN), :].T
    dk_ref[...] = jnp.zeros(dk_ref.shape, F32)
    dv_ref[...] = jnp.zeros(dv_ref.shape, F32)
    if first:
        dqt_ref[...] = jnp.zeros(dqt_ref.shape, F32)
    else:
        dqt_ref[...] = dqt_in[...]

    def begin(a, q_which, b, k_which, masked):
        slot = a * 2 + q_which
        q_ref, base = source
        queries = half(q_ref, a - base, q_which, 0)
        out_grads = half(q_ref, a - base, q_which, 1)
        i = pieces.index(b)
        scores = lax.dot_general(
            half(kv_ref, i, k_which, 0), queries, NT, preferred_element_type=F32
        ) * SCALE2
        dprobs = lax.dot_general(
            half(kv_ref, i, k_which, 1), out_grads, NT, preferred_element_type=F32
        )
        return slot, 2 * i + k_which, masked, queries, out_grads, scores, dprobs

    def finish(state):
        slot, key_slot, masked, queries, out_grads, scores, dprobs = state
        probs = jnp.exp2(scores.reshape(32, 8, SPAN) - norm_ref[slot][None])
        if masked:
            probs = jnp.where(diagonal_visible().reshape(32, 8, SPAN), probs, 0.0)
        dscores = probs * (dprobs.reshape(32, 8, SPAN) - delta_ref[slot][None])
        probs = probs.reshape(SPAN, SPAN).astype(BF16)
        dscores = dscores.reshape(SPAN, SPAN).astype(BF16)
        dv_ref[key_slot] += lax.dot_general(probs, out_grads, NN, preferred_element_type=F32)
        dk_ref[key_slot] += lax.dot_general(dscores, queries, NN, preferred_element_type=F32)
        dqt_ref[slot] += lax.dot_general(kt_ref[key_slot], dscores, NN, preferred_element_type=F32)

    tile, drain = in_flight(begin, finish, 1)
    for source in ((near_ref, 0), (far_ref, 4)):
        for a in range(source[1], source[1] + 4):
            one_query_piece(order_ref, tile, a, pieces, a == 0 and 0 in pieces)
    drain()
    parts = [ref for i in range(len(pieces)) for ref in (dk_ref.at[2 * i], dk_ref.at[2 * i + 1], dv_ref.at[2 * i], dv_ref.at[2 * i + 1])]
    for ref in dkv_refs:
        for j in range(ref.shape[0] // SPAN):
            ref[pl.ds(j * SPAN, SPAN), :] = parts.pop(0)[...].astype(ref.dtype)
    if last:
        for out, first_slot in zip(dq_outs, (0, 8)):
            out[...] = dqt_ref[first_slot : first_slot + 8].astype(out.dtype)


def pack_kernel(queries_ref, keys_ref, values_ref, grads_ref, q_ref, kv_ref, sems):
    rows = 2 * SPAN
    copies = []
    for i, (source, target) in enumerate(
        ((queries_ref, q_ref), (grads_ref, q_ref), (keys_ref, kv_ref), (values_ref, kv_ref))
    ):
        place = target.at[pl.ds((i % 2) * rows, rows), :]
        copies.append(pltpu.make_async_copy(source, place, sems.at[i]))
    for copy in copies:
        copy.start()
    for copy in copies:
        copy.wait()


def relay_kernel(dkv1_ref, dkv3_ref, keys_ref, values_ref, out1_ref, out3_ref):
    keys, values = pl.ds(0, 2 * SPAN), pl.ds(2 * SPAN, 2 * SPAN)
    out1_ref[keys, :] = (dkv1_ref[keys, :] + keys_ref[...].astype(F32)).astype(BF16)
    out1_ref[values, :] = dkv1_ref[values, :].astype(BF16)
    out3_ref[keys, :] = dkv3_ref[keys, :].astype(BF16)
    out3_ref[values, :] = (dkv3_ref[values, :] + values_ref[...].astype(F32)).astype(BF16)


def middle_kernel(dkv_ref, z1_ref, z3_ref, sum_ref):
    total = dkv_ref[...] + z1_ref[...].astype(F32) + z3_ref[...].astype(F32)
    sum_ref[...] = total.astype(BF16)


def query_kernel(keep_ref, other_ref, dq_ref, r1_ref, r3_ref, first_ref, second_ref):
    for k, ref in ((0, dq_ref), (1, r1_ref), (3, r3_ref)):
        slots = pl.ds(2 * k, 2)
        ref[...] = keep_ref[slots] + other_ref[slots].astype(F32)
    for slot, ref in ((4, first_ref), (5, second_ref)):
        ref[...] = (keep_ref[slot] + other_ref[slot].astype(F32)).astype(BF16)


def query_relay_kernel(r1_ref, r3_ref, first_ref, second_ref, out1_ref, out3_ref):
    out1_ref[0] = (r1_ref[0] + first_ref[...].astype(F32)).astype(BF16)
    out1_ref[1] = r1_ref[1].astype(BF16)
    out3_ref[0] = r3_ref[0].astype(BF16)
    out3_ref[1] = (r3_ref[1] + second_ref[...].astype(F32)).astype(BF16)


def last_kernel(sum_ref, x1_ref, x2_ref, x3_ref, dq_ref, y1_ref, y3_ref, q_out, k_out, v_out):
    own, x1, x2, x3 = [ref[...].astype(F32) for ref in (sum_ref, x1_ref, x2_ref, x3_ref)]
    total = (own + x2) + (x1 + x3)
    k_out[...] = (total[: 2 * SPAN] * SCALE).astype(BF16)
    v_out[...] = total[2 * SPAN :].astype(BF16)
    dq = dq_ref[...]
    for ref in (y1_ref, y3_ref):
        dq = dq + ref[...].astype(F32)
    for slot in range(2):
        q_out[pl.ds(slot * SPAN, SPAN), :] = (dq[slot] * SCALE).T.astype(BF16)


SMEM = pl.BlockSpec(memory_space=pltpu.SMEM)
VMEM = pl.BlockSpec(memory_space=pltpu.VMEM)
PIECE = 4 * SPAN


def call_stats(far, span_order, q_pieces, kvs, *before):
    args = [span_order, q_pieces.reshape(4, PIECE, DH), *kvs, *before]
    return pl.pallas_call(
        functools.partial(stats_kernel, far),
        out_shape=jax.ShapeDtypeStruct((3, 16, SPAN), F32),
        in_specs=[SMEM] + [VMEM] * (len(args) - 1),
        out_specs=VMEM,
        scratch_shapes=[pltpu.VMEM((4, PIECE, DH), BF16)] + [pltpu.VMEM((8, 8, SPAN), F32)] * 3,
        compiler_params=pltpu.CompilerParams(vmem_limit_bytes=32 * 2**20),
        cost_estimate=pl.CostEstimate(
            flops=32 * 2 * 2 * SPAN * SPAN * DH, bytes_accessed=2**21, transcendentals=32 * SPAN * SPAN
        ),
        name="stats",
    )(*args)


def dkv_parts(pieces):
    if pieces == (2,):
        return (jax.ShapeDtypeStruct((PIECE // 2, DH), BF16),) * 2
    return (jax.ShapeDtypeStruct((PIECE, DH), F32),) * len(pieces)


def call_grads(pieces, first, last, span_order, stats, q_near, q_far, kvs, dqt):
    tiles = 16 * len(pieces)
    dkv_shapes = dkv_parts(pieces)
    if last:
        dq_shapes = tuple(jax.ShapeDtypeStruct((8, DH, SPAN), dtype) for dtype in (F32, BF16))
    else:
        dq_shapes = (jax.ShapeDtypeStruct((16, DH, SPAN), F32),)
    q_pieces = [q.reshape(4, PIECE, DH) for q in (q_near, q_far)]
    args = [span_order, *stats, *q_pieces, *[kvs[b] for b in pieces]] + ([] if first else [dqt])
    out = pl.pallas_call(
        functools.partial(grads_kernel, pieces, first, last),
        out_shape=dkv_shapes + dq_shapes,
        in_specs=[SMEM] + [VMEM] * (len(args) - 1),
        out_specs=(VMEM,) * (len(dkv_shapes) + len(dq_shapes)),
        scratch_shapes=[
            pltpu.VMEM((len(pieces), PIECE, DH), BF16),
            pltpu.VMEM((2, 16, SPAN), F32),
            pltpu.VMEM((16, 8, SPAN), F32),
            pltpu.VMEM((16, 8, SPAN), F32),
            pltpu.VMEM((2 * len(pieces), SPAN, DH), F32),
            pltpu.VMEM((2 * len(pieces), SPAN, DH), F32),
            pltpu.VMEM((2 * len(pieces), DH, SPAN), BF16),
        ]
        + ([pltpu.VMEM((16, DH, SPAN), F32)] if last else []),
        compiler_params=pltpu.CompilerParams(vmem_limit_bytes=32 * 2**20),
        cost_estimate=pl.CostEstimate(
            flops=tiles * 5 * 2 * SPAN * SPAN * DH, bytes_accessed=4 * 2**20, transcendentals=tiles * SPAN * SPAN
        ),
        name="grads",
    )(*args)
    return out[: len(dkv_shapes)], out[len(dkv_shapes) :]


def plain_call(kernel, name, out_shapes, *args):
    return pl.pallas_call(
        kernel,
        out_shape=tuple(jax.ShapeDtypeStruct(shape, dtype) for shape, dtype in out_shapes),
        in_specs=[VMEM] * len(args),
        out_specs=(VMEM,) * len(out_shapes),
        compiler_params=pltpu.CompilerParams(vmem_limit_bytes=16 * 2**20),
        cost_estimate=pl.CostEstimate(flops=2**20, bytes_accessed=2**21, transcendentals=0),
        name=name,
    )(*args)


def call_pack(*args):
    return pl.pallas_call(
        pack_kernel,
        out_shape=(jax.ShapeDtypeStruct((PIECE, DH), BF16),) * 2,
        in_specs=[pl.BlockSpec(memory_space=pl.ANY)] * 4,
        out_specs=(VMEM, VMEM),
        scratch_shapes=[pltpu.SemaphoreType.DMA((4,))],
        compiler_params=pltpu.CompilerParams(vmem_limit_bytes=56 * 2**20),
        name="pack",
    )(*args)


def back(value, axis, k):
    return lax.ppermute(value, axis, [(i, (i + k) % 4) for i in range(4)])


def ahead(value, axis, k):
    return lax.ppermute(value, axis, [(i, (i - k) % 4) for i in range(4)])


def swap_core(value):
    return lax.ppermute(value, "c", [(0, 1), (1, 0)])


def merged(mine, theirs):
    top = jnp.maximum(mine[0], theirs[0])
    mine_by, theirs_by = jnp.exp2(mine[0] - top), jnp.exp2(theirs[0] - top)
    return jnp.stack([top, mine[1] * mine_by + theirs[1] * theirs_by, mine[2] * mine_by + theirs[2] * theirs_by])


def local(span_order, queries, key_rows, value_rows, out_grads):
    q_own, kv_own = call_pack(queries, key_rows, value_rows, out_grads)
    q_got = [back(q_own, "y", k) for k in (1, 2, 3)]
    kv1, kv3 = back(kv_own, "z", 1), back(kv_own, "z", 3)
    kv_again, kv1, kv3 = lax.optimization_barrier((kv_own, kv1, kv3))
    kv2 = back(kv_again, "z", 2)
    q_got, kv2 = lax.optimization_barrier((q_got, kv2))
    q_near = jnp.concatenate([q_own] + q_got, axis=0)
    q_far = swap_core(q_near)
    kvs = [kv_own, kv1, kv2, kv3]

    stats = call_stats(False, span_order, q_near, kvs)
    stats = call_stats(True, span_order, q_far, kvs, stats)
    stats = merged(stats, swap_core(stats))
    total = jnp.maximum(stats[1], TINY)
    stats = jnp.stack([stats[0] + jnp.log2(total), stats[2] / total])
    stats = [stats] + [back(stats, "y", k) for k in (1, 2, 3)]

    common = (span_order, stats, q_near, q_far, kvs)
    (dk2, dv2), (dqt,) = call_grads((2,), True, False, *common, None)
    dk_relay, dv_relay = ahead(dk2, "z", 1), ahead(dv2, "z", 3)
    (dkv1, dkv3), (dqt,) = call_grads((1, 3), False, False, *common, dqt)
    dkv1, dkv3 = plain_call(relay_kernel, "relay", [((PIECE, DH), BF16)] * 2, dkv1, dkv3, dk_relay, dv_relay)
    (dkv0,), (dq_keep, dq_send) = call_grads((0,), False, True, *common, dqt)
    z1, z3 = ahead(dkv1, "z", 1), ahead(dkv3, "z", 3)
    (summed,) = plain_call(middle_kernel, "middle", [((PIECE, DH), BF16)], dkv0, z1, z3)
    dq_send, summed = lax.optimization_barrier((dq_send, summed))
    dq_other = swap_core(dq_send)
    rows, slots = (2 * SPAN, DH), (2, DH, SPAN)
    one = (DH, SPAN)
    dq, r1, r3, first, second = plain_call(
        query_kernel, "query", [(slots, F32)] * 3 + [(one, BF16)] * 2, dq_keep, dq_other
    )
    r1, r3 = plain_call(
        query_relay_kernel, "query_relay", [(slots, BF16)] * 2, r1, r3, ahead(first, "y", 1), ahead(second, "y", 3)
    )
    xs = [back(summed, "x", k) for k in (1, 2, 3)]
    ys = [ahead(r1, "y", 1), ahead(r3, "y", 3)]
    return plain_call(last_kernel, "last", [(rows, BF16)] * 3, summed, *xs, dq, *ys)


def solution(mesh):
    fine = Mesh(mesh.devices.reshape(4, 4, 2, 4), ("z", "y", "c", "x"))
    ctx = ("z", "y", "c")
    return jax.shard_map(
        local,
        mesh=fine,
        in_specs=(P(), P(ctx, "x"), P(ctx, None), P(ctx, None), P(ctx, "x")),
        out_specs=(P(ctx, "x"), P(ctx, None), P(ctx, None)),
        check_vma=False,
    )
```

```python
import functools

import jax
import jax.numpy as jnp
from jax import lax
from jax.experimental import pallas as pl
from jax.experimental.pallas import tpu as pltpu
from jax.sharding import Mesh, PartitionSpec as P

DH = 128
SPAN = 256
SCALE = DH ** (-0.5)
LOG2E = 1.4426950408889634
SCALE2 = SCALE * LOG2E
NEG = -1e30
TINY = 1e-30
NT = (((1,), (1,)), ((), ()))
NN = (((1,), (0,)), ((), ()))
F32 = jnp.float32
BF16 = jnp.bfloat16


def spans_of(order_ref, z, y, c):
    row = (z * 4 + y) * 2 + c
    first, second = order_ref[row, 0], order_ref[row, 1]
    return jnp.minimum(first, second), jnp.where(first < second, 0, 1)


def query_spans(order_ref, a):
    z, y, c = lax.axis_index("z"), lax.axis_index("y"), lax.axis_index("c")
    return spans_of(order_ref, z, (y + 4 - a % 4) % 4, (c + a // 4) % 2)


def key_spans(order_ref, b):
    z, y, c = lax.axis_index("z"), lax.axis_index("y"), lax.axis_index("c")
    return spans_of(order_ref, (z + 4 - b) % 4, y, c)


def one_query_piece(order_ref, tile, a, pieces, own):
    low, low_slot = query_spans(order_ref, a)
    found = [key_spans(order_ref, b) for b in pieces]
    tile(a, 1 - low_slot, [(b, slot) for b, (_, slot) in zip(pieces, found)], False)
    for b, (key_low, key_slot) in zip(pieces, found):
        if own and b == 0:
            tile(0, 0, [(0, 0)], True)
            tile(0, 1, [(0, 1)], True)
        else:
            lows = low > key_low
            tile(a, jnp.where(lows, low_slot, 1 - low_slot), [(b, jnp.where(lows, key_slot, 1 - key_slot))], False)


def half(ref, piece, which, second):
    begin = which * SPAN + second * 2 * SPAN
    if not isinstance(begin, int):
        begin = pl.multiple_of(begin, SPAN)
    return ref[piece, pl.ds(begin, SPAN), :]


def products(q_ref, kv_ref, a, q_which, b, k_which):
    scores = lax.dot_general(
        half(kv_ref, b, k_which, 0), half(q_ref, a, q_which, 0), NT, preferred_element_type=F32
    )
    dprobs = lax.dot_general(
        half(kv_ref, b, k_which, 1), half(q_ref, a, q_which, 1), NT, preferred_element_type=F32
    )
    return scores * SCALE2, dprobs


def diagonal_visible():
    key_row = lax.broadcasted_iota(jnp.int32, (SPAN, SPAN), 0)
    query_row = lax.broadcasted_iota(jnp.int32, (SPAN, SPAN), 1)
    return key_row <= query_row


def query_place(a):
    y, c = lax.axis_index("y"), lax.axis_index("c")
    return 2 * (((y + 4 - a % 4) % 4) * 2 + (c + a // 4) % 2)


def in_flight(begin, finish, depth):
    waiting = []

    def tile(a, q_which, keys, masked):
        for b, k_which in keys:
            waiting.append(begin(a, q_which, b, k_which, masked))
            if len(waiting) > depth:
                finish(waiting.pop(0))

    def drain():
        while waiting:
            finish(waiting.pop(0))

    return tile, drain


def stats_kernel(far, order_ref, q_ref, *refs):
    kv_refs, refs = refs[:4], refs[4:]
    if far:
        before_ref, refs = refs[0], refs[1:]
    out_ref, kv_ref, top_ref, total_ref, weighted_ref = refs
    if far:
        out_ref[...] = before_ref[...]
    for b, ref in enumerate(kv_refs):
        kv_ref[b] = ref[...]
    top_ref[...] = jnp.full(top_ref.shape, NEG, F32)
    total_ref[...] = jnp.zeros(total_ref.shape, F32)
    weighted_ref[...] = jnp.zeros(weighted_ref.shape, F32)
    base = 4 if far else 0
    pieces = (0, 1, 2, 3)

    def begin(a, q_which, b, k_which, masked):
        scores, dprobs = products(q_ref, kv_ref, a - base, q_which, b, k_which)
        if masked:
            scores = jnp.where(diagonal_visible(), scores, NEG)
        return (a - base) * 2 + q_which, masked, scores.reshape(32, 8, SPAN), dprobs.reshape(32, 8, SPAN)

    def finish(state):
        slot, masked, scores, dprobs = state
        old = top_ref[slot]
        top = jnp.maximum(old, jnp.max(scores, axis=0))
        shrink = jnp.exp2(old - top)
        expon = jnp.exp2(scores - top[None])
        if masked:
            expon = jnp.where(diagonal_visible().reshape(32, 8, SPAN), expon, 0.0)
        top_ref[slot] = top
        total_ref[slot] = total_ref[slot] * shrink + jnp.sum(expon, axis=0)
        weighted_ref[slot] = weighted_ref[slot] * shrink + jnp.sum(expon * dprobs, axis=0)

    tile, drain = in_flight(begin, finish, 2)
    for a in range(base, base + 4):
        one_query_piece(order_ref, tile, a, pieces, a == 0)
    drain()
    for slot in range(8):
        tops = top_ref[slot]
        top = jnp.max(tops, axis=0, keepdims=True)
        factor = jnp.exp2(tops - top)
        total = jnp.maximum(jnp.sum(total_ref[slot] * factor, axis=0, keepdims=True), TINY)
        weighted = jnp.sum(weighted_ref[slot] * factor, axis=0, keepdims=True)
        rows = (top + jnp.log2(total), weighted / total)
        place = query_place(base + slot // 2) + slot % 2
        for kind, row in enumerate(rows):
            out_ref[kind, pl.ds(place, 1), :] = row


def norm_and_delta(stat_refs, sum_ref, norm_ref, delta_ref):
    found = [(ref[0], ref[1]) for ref in stat_refs]
    top = functools.reduce(jnp.maximum, [norm for norm, _ in found])
    factors = [jnp.exp2(norm - top) for norm, _ in found]
    total = sum(factors)
    sum_ref[0] = top + jnp.log2(total)
    sum_ref[1] = sum(delta * g for (_, delta), g in zip(found, factors)) / total
    for slot in range(16):
        place = query_place(slot // 2) + slot % 2
        norm_ref[slot] = jnp.broadcast_to(sum_ref[0, pl.ds(place, 1), :], (8, SPAN))
        delta_ref[slot] = jnp.broadcast_to(sum_ref[1, pl.ds(place, 1), :], (8, SPAN))


def grads_kernel(pieces, first, last, *refs):
    refs = list(refs)
    order_ref, stat_refs, near_ref, far_ref = refs[0], refs[1:5], refs[5], refs[6]
    del refs[:7]
    kv_refs = refs[: len(pieces)]
    del refs[: len(pieces)]
    dqt_in = None if first else refs.pop(0)
    dkv_refs = [refs.pop(0) for _ in dkv_parts(pieces)]
    dq_outs = [refs.pop(0), refs.pop(0)] if last else [refs.pop(0)]
    kv_ref, sum_ref, norm_ref, delta_ref, dk_ref, dv_ref, kt_ref = refs[:7]
    dqt_ref = refs[7] if last else dq_outs[0]

    norm_and_delta(stat_refs, sum_ref, norm_ref, delta_ref)
    for i, b in enumerate(pieces):
        kv_ref[i] = kv_refs[i][...]
        for which in range(2):
            kt_ref[2 * i + which] = kv_ref[i, pl.ds(which * SPAN, SPAN), :].T
    dk_ref[...] = jnp.zeros(dk_ref.shape, F32)
    dv_ref[...] = jnp.zeros(dv_ref.shape, F32)
    if first:
        dqt_ref[...] = jnp.zeros(dqt_ref.shape, F32)
    else:
        dqt_ref[...] = dqt_in[...]

    def begin(a, q_which, b, k_which, masked):
        slot = a * 2 + q_which
        q_ref, base = source
        queries = half(q_ref, a - base, q_which, 0)
        out_grads = half(q_ref, a - base, q_which, 1)
        i = pieces.index(b)
        scores = lax.dot_general(
            half(kv_ref, i, k_which, 0), queries, NT, preferred_element_type=F32
        ) * SCALE2
        dprobs = lax.dot_general(
            half(kv_ref, i, k_which, 1), out_grads, NT, preferred_element_type=F32
        )
        return slot, 2 * i + k_which, masked, queries, out_grads, scores, dprobs

    def finish(state):
        slot, key_slot, masked, queries, out_grads, scores, dprobs = state
        probs = jnp.exp2(scores.reshape(32, 8, SPAN) - norm_ref[slot][None])
        if masked:
            probs = jnp.where(diagonal_visible().reshape(32, 8, SPAN), probs, 0.0)
        dscores = probs * (dprobs.reshape(32, 8, SPAN) - delta_ref[slot][None])
        probs = probs.reshape(SPAN, SPAN).astype(BF16)
        dscores = dscores.reshape(SPAN, SPAN).astype(BF16)
        dv_ref[key_slot] += lax.dot_general(probs, out_grads, NN, preferred_element_type=F32)
        dk_ref[key_slot] += lax.dot_general(dscores, queries, NN, preferred_element_type=F32)
        dqt_ref[slot] += lax.dot_general(kt_ref[key_slot], dscores, NN, preferred_element_type=F32)

    tile, drain = in_flight(begin, finish, 1)
    for source in ((near_ref, 0), (far_ref, 4)):
        for a in range(source[1], source[1] + 4):
            one_query_piece(order_ref, tile, a, pieces, a == 0 and 0 in pieces)
    drain()
    parts = [ref for i in range(len(pieces)) for ref in (dk_ref.at[2 * i], dk_ref.at[2 * i + 1], dv_ref.at[2 * i], dv_ref.at[2 * i + 1])]
    for ref in dkv_refs:
        for j in range(ref.shape[0] // SPAN):
            ref[pl.ds(j * SPAN, SPAN), :] = parts.pop(0)[...].astype(ref.dtype)
    if last:
        for out, first_slot in zip(dq_outs, (0, 8)):
            out[...] = dqt_ref[first_slot : first_slot + 8].astype(out.dtype)


def pack_kernel(queries_ref, keys_ref, values_ref, grads_ref, q_ref, kv_ref, sems):
    rows = 2 * SPAN
    copies = []
    for i, (source, target) in enumerate(
        ((queries_ref, q_ref), (grads_ref, q_ref), (keys_ref, kv_ref), (values_ref, kv_ref))
    ):
        place = target.at[pl.ds((i % 2) * rows, rows), :]
        copies.append(pltpu.make_async_copy(source, place, sems.at[i]))
    for copy in copies:
        copy.start()
    for copy in copies:
        copy.wait()


def relay_kernel(dkv1_ref, dkv3_ref, keys_ref, values_ref, out1_ref, out3_ref):
    keys, values = pl.ds(0, 2 * SPAN), pl.ds(2 * SPAN, 2 * SPAN)
    out1_ref[keys, :] = (dkv1_ref[keys, :] + keys_ref[...].astype(F32)).astype(BF16)
    out1_ref[values, :] = dkv1_ref[values, :].astype(BF16)
    out3_ref[keys, :] = dkv3_ref[keys, :].astype(BF16)
    out3_ref[values, :] = (dkv3_ref[values, :] + values_ref[...].astype(F32)).astype(BF16)


def middle_kernel(dkv_ref, z1_ref, z3_ref, sum_ref):
    total = dkv_ref[...] + z1_ref[...].astype(F32) + z3_ref[...].astype(F32)
    sum_ref[...] = total.astype(BF16)


def query_kernel(keep_ref, other_ref, dq_ref, r1_ref, r3_ref, first_ref, second_ref):
    for k, ref in ((0, dq_ref), (1, r1_ref), (3, r3_ref)):
        slots = pl.ds(2 * k, 2)
        ref[...] = keep_ref[slots] + other_ref[slots].astype(F32)
    for slot, ref in ((4, first_ref), (5, second_ref)):
        ref[...] = (keep_ref[slot] + other_ref[slot].astype(F32)).astype(BF16)


def query_relay_kernel(r1_ref, r3_ref, first_ref, second_ref, out1_ref, out3_ref):
    out1_ref[0] = (r1_ref[0] + first_ref[...].astype(F32)).astype(BF16)
    out1_ref[1] = r1_ref[1].astype(BF16)
    out3_ref[0] = r3_ref[0].astype(BF16)
    out3_ref[1] = (r3_ref[1] + second_ref[...].astype(F32)).astype(BF16)


def last_kernel(sum_ref, x1_ref, x2_ref, x3_ref, dq_ref, y1_ref, y3_ref, q_out, k_out, v_out):
    own, x1, x2, x3 = [ref[...].astype(F32) for ref in (sum_ref, x1_ref, x2_ref, x3_ref)]
    total = (own + x2) + (x1 + x3)
    k_out[...] = (total[: 2 * SPAN] * SCALE).astype(BF16)
    v_out[...] = total[2 * SPAN :].astype(BF16)
    dq = dq_ref[...]
    for ref in (y1_ref, y3_ref):
        dq = dq + ref[...].astype(F32)
    for slot in range(2):
        q_out[pl.ds(slot * SPAN, SPAN), :] = (dq[slot] * SCALE).T.astype(BF16)


SMEM = pl.BlockSpec(memory_space=pltpu.SMEM)
VMEM = pl.BlockSpec(memory_space=pltpu.VMEM)
PIECE = 4 * SPAN


def call_stats(far, span_order, q_pieces, kvs, *before):
    args = [span_order, q_pieces.reshape(4, PIECE, DH), *kvs, *before]
    return pl.pallas_call(
        functools.partial(stats_kernel, far),
        out_shape=jax.ShapeDtypeStruct((2, 16, SPAN), F32),
        in_specs=[SMEM] + [VMEM] * (len(args) - 1),
        out_specs=VMEM,
        scratch_shapes=[pltpu.VMEM((4, PIECE, DH), BF16)] + [pltpu.VMEM((8, 8, SPAN), F32)] * 3,
        compiler_params=pltpu.CompilerParams(vmem_limit_bytes=32 * 2**20),
        cost_estimate=pl.CostEstimate(
            flops=32 * 2 * 2 * SPAN * SPAN * DH, bytes_accessed=2**21, transcendentals=32 * SPAN * SPAN
        ),
        name="stats",
    )(*args)


def dkv_parts(pieces):
    if pieces == (2,):
        return (jax.ShapeDtypeStruct((PIECE // 2, DH), BF16),) * 2
    return (jax.ShapeDtypeStruct((PIECE, DH), F32),) * len(pieces)


def call_grads(pieces, first, last, span_order, stats, q_near, q_far, kvs, dqt):
    tiles = 16 * len(pieces)
    dkv_shapes = dkv_parts(pieces)
    if last:
        dq_shapes = tuple(jax.ShapeDtypeStruct((8, DH, SPAN), dtype) for dtype in (F32, BF16))
    else:
        dq_shapes = (jax.ShapeDtypeStruct((16, DH, SPAN), F32),)
    q_pieces = [q.reshape(4, PIECE, DH) for q in (q_near, q_far)]
    args = [span_order, *stats, *q_pieces, *[kvs[b] for b in pieces]] + ([] if first else [dqt])
    out = pl.pallas_call(
        functools.partial(grads_kernel, pieces, first, last),
        out_shape=dkv_shapes + dq_shapes,
        in_specs=[SMEM] + [VMEM] * (len(args) - 1),
        out_specs=(VMEM,) * (len(dkv_shapes) + len(dq_shapes)),
        scratch_shapes=[
            pltpu.VMEM((len(pieces), PIECE, DH), BF16),
            pltpu.VMEM((2, 16, SPAN), F32),
            pltpu.VMEM((16, 8, SPAN), F32),
            pltpu.VMEM((16, 8, SPAN), F32),
            pltpu.VMEM((2 * len(pieces), SPAN, DH), F32),
            pltpu.VMEM((2 * len(pieces), SPAN, DH), F32),
            pltpu.VMEM((2 * len(pieces), DH, SPAN), BF16),
        ]
        + ([pltpu.VMEM((16, DH, SPAN), F32)] if last else []),
        compiler_params=pltpu.CompilerParams(vmem_limit_bytes=32 * 2**20),
        cost_estimate=pl.CostEstimate(
            flops=tiles * 5 * 2 * SPAN * SPAN * DH, bytes_accessed=4 * 2**20, transcendentals=tiles * SPAN * SPAN
        ),
        name="grads",
    )(*args)
    return out[: len(dkv_shapes)], out[len(dkv_shapes) :]


def plain_call(kernel, name, out_shapes, *args):
    return pl.pallas_call(
        kernel,
        out_shape=tuple(jax.ShapeDtypeStruct(shape, dtype) for shape, dtype in out_shapes),
        in_specs=[VMEM] * len(args),
        out_specs=(VMEM,) * len(out_shapes),
        compiler_params=pltpu.CompilerParams(vmem_limit_bytes=16 * 2**20),
        cost_estimate=pl.CostEstimate(flops=2**20, bytes_accessed=2**21, transcendentals=0),
        name=name,
    )(*args)


def call_pack(*args):
    return pl.pallas_call(
        pack_kernel,
        out_shape=(jax.ShapeDtypeStruct((PIECE, DH), BF16),) * 2,
        in_specs=[pl.BlockSpec(memory_space=pl.ANY)] * 4,
        out_specs=(VMEM, VMEM),
        scratch_shapes=[pltpu.SemaphoreType.DMA((4,))],
        compiler_params=pltpu.CompilerParams(vmem_limit_bytes=56 * 2**20),
        name="pack",
    )(*args)


def back(value, axis, k):
    return lax.ppermute(value, axis, [(i, (i + k) % 4) for i in range(4)])


def ahead(value, axis, k):
    return lax.ppermute(value, axis, [(i, (i - k) % 4) for i in range(4)])


def swap_core(value):
    return lax.ppermute(value, "c", [(0, 1), (1, 0)])


def merged(mine, theirs):
    top = jnp.maximum(mine[0], theirs[0])
    mine_by, theirs_by = jnp.exp2(mine[0] - top), jnp.exp2(theirs[0] - top)
    total = mine_by + theirs_by
    return jnp.stack([top + jnp.log2(total), (mine[1] * mine_by + theirs[1] * theirs_by) / total])


def local(span_order, queries, key_rows, value_rows, out_grads):
    q_own, kv_own = call_pack(queries, key_rows, value_rows, out_grads)
    q_got = [back(q_own, "y", k) for k in (1, 2, 3)]
    kv1, kv3 = back(kv_own, "z", 1), back(kv_own, "z", 3)
    kv_again, kv1, kv3 = lax.optimization_barrier((kv_own, kv1, kv3))
    kv2 = back(kv_again, "z", 2)
    q_got, kv2 = lax.optimization_barrier((q_got, kv2))
    q_near = jnp.concatenate([q_own] + q_got, axis=0)
    q_far = swap_core(q_near)
    kvs = [kv_own, kv1, kv2, kv3]

    stats = call_stats(False, span_order, q_near, kvs)
    stats = call_stats(True, span_order, q_far, kvs, stats)
    stats = merged(stats, swap_core(stats))
    stats = [stats] + [back(stats, "y", k) for k in (1, 2, 3)]

    common = (span_order, stats, q_near, q_far, kvs)
    (dk2, dv2), (dqt,) = call_grads((2,), True, False, *common, None)
    dk_relay, dv_relay = ahead(dk2, "z", 1), ahead(dv2, "z", 3)
    (dkv1, dkv3), (dqt,) = call_grads((1, 3), False, False, *common, dqt)
    dkv1, dkv3 = plain_call(relay_kernel, "relay", [((PIECE, DH), BF16)] * 2, dkv1, dkv3, dk_relay, dv_relay)
    (dkv0,), (dq_keep, dq_send) = call_grads((0,), False, True, *common, dqt)
    z1, z3 = ahead(dkv1, "z", 1), ahead(dkv3, "z", 3)
    (summed,) = plain_call(middle_kernel, "middle", [((PIECE, DH), BF16)], dkv0, z1, z3)
    dq_send, summed = lax.optimization_barrier((dq_send, summed))
    dq_other = swap_core(dq_send)
    rows, slots = (2 * SPAN, DH), (2, DH, SPAN)
    one = (DH, SPAN)
    dq, r1, r3, first, second = plain_call(
        query_kernel, "query", [(slots, F32)] * 3 + [(one, BF16)] * 2, dq_keep, dq_other
    )
    r1, r3 = plain_call(
        query_relay_kernel, "query_relay", [(slots, BF16)] * 2, r1, r3, ahead(first, "y", 1), ahead(second, "y", 3)
    )
    xs = [back(summed, "x", k) for k in (1, 2, 3)]
    ys = [ahead(r1, "y", 1), ahead(r3, "y", 3)]
    return plain_call(last_kernel, "last", [(rows, BF16)] * 3, summed, *xs, dq, *ys)


def solution(mesh):
    fine = Mesh(mesh.devices.reshape(4, 4, 2, 4), ("z", "y", "c", "x"))
    ctx = ("z", "y", "c")
    return jax.shard_map(
        local,
        mesh=fine,
        in_specs=(P(), P(ctx, "x"), P(ctx, None), P(ctx, None), P(ctx, "x")),
        out_specs=(P(ctx, "x"), P(ctx, None), P(ctx, None)),
        check_vma=False,
    )
```
